32 devices in a mesh: dp: 16 (over z, y, x), tensor: 2 (over core).
Axes of the slice: x: 2, y: 2, z: 4, core: 2. Of those that a mesh axis runs over, the one named last changes fastest.
Arguments:
- inputs: bfloat16 [16, 512, 768], P('dp'), may hold values from -6 to 6
- datastore: bfloat16 [16, 2048, 768], P('dp'), may hold values from -6 to 6
- lengths: int32 [16], P('dp'), may hold values from 64 to 512, as said below
- indices: int32 [16, 512, 1024], P('dp'), may hold values from 0 to 2047, as said below
- w_query: bfloat16 [768, 768], P(None, 'tensor'), may hold values from -0.21875 to 0.21875
- b_query: bfloat16 [768], P('tensor'), may hold values from -2 to 2
- w_key: bfloat16 [768, 768], P(None, 'tensor'), may hold values from -0.21875 to 0.21875
- w_value: bfloat16 [768, 768], P(None, 'tensor'), may hold values from -0.21875 to 0.21875
- b_value: bfloat16 [768], P('tensor'), may hold values from -0.5 to 0.5
- w_out: bfloat16 [768, 768], P('tensor'), may hold values from -2.5 to 2.5
- b_out: bfloat16 [768], replicated, may hold values from -2 to 2
- g_one: bfloat16 [768], replicated, may hold values from 0.5 to 1.5
- c_one: bfloat16 [768], replicated, may hold values from -2 to 2
- wc_query: bfloat16 [768, 768], P(None, 'tensor'), may hold values from -0.21875 to 0.21875
- bc_query: bfloat16 [768], P('tensor'), may hold values from -2 to 2
- wc_key: bfloat16 [768, 768], P(None, 'tensor'), may hold values from -0.21875 to 0.21875
- wc_value: bfloat16 [768, 768], P(None, 'tensor'), may hold values from -0.21875 to 0.21875
- bc_value: bfloat16 [768], P('tensor'), may hold values from -0.5 to 0.5
- wc_out: bfloat16 [768, 768], P('tensor'), may hold values from -3.5 to 3.5
- bc_out: bfloat16 [768], replicated, may hold values from -2 to 2
- g_two: bfloat16 [768], replicated, may hold values from 0.5 to 1.5
- c_two: bfloat16 [768], replicated, may hold values from -2 to 2
- w_up: bfloat16 [768, 3072], P(None, 'tensor'), may hold values from -0.21875 to 0.21875
- b_up: bfloat16 [3072], P('tensor'), may hold values from -3 to 3
- w_down: bfloat16 [3072, 768], P('tensor'), may hold values from -0.21875 to 0.21875
- b_down: bfloat16 [768], replicated, may hold values from -2 to 2
- g_three: bfloat16 [768], replicated, may hold values from 0.5 to 1.5
- c_three: bfloat16 [768], replicated, may hold values from -2 to 2
- cotangent: bfloat16 [16, 512, 768], P('dp'), may hold values from -6 to 6
Outputs:
- output: bfloat16 [16, 512, 768], P('dp')
- input_grad: float32 [16, 512, 768], P('dp')
- datastore_grad: float32 [16, 2048, 768], P('dp', 'tensor')
- grad_w_query: float32 [768, 768], P('dp', 'tensor')
- grad_b_query: float32 [768], P(('tensor', 'dp'))
- grad_w_key: float32 [768, 768], P('dp', 'tensor')
- grad_w_value: float32 [768, 768], P('dp', 'tensor')
- grad_b_value: float32 [768], P(('tensor', 'dp'))
- grad_w_out: float32 [768, 768], P('tensor', 'dp')
- grad_b_out: float32 [768], P('dp')
- grad_g_one: float32 [768], P('dp')
- grad_c_one: float32 [768], P('dp')
- grad_wc_query: float32 [768, 768], P('dp', 'tensor')
- grad_bc_query: float32 [768], P(('tensor', 'dp'))
- grad_wc_key: float32 [768, 768], P('dp', 'tensor')
- grad_wc_value: float32 [768, 768], P('dp', 'tensor')
- grad_bc_value: float32 [768], P(('tensor', 'dp'))
- grad_wc_out: float32 [768, 768], P('tensor', 'dp')
- grad_bc_out: float32 [768], P('dp')
- grad_g_two: float32 [768], P('dp')
- grad_c_two: float32 [768], P('dp')
- grad_w_up: float32 [768, 3072], P('dp', 'tensor')
- grad_b_up: float32 [3072], P(('tensor', 'dp'))
- grad_w_down: float32 [3072, 768], P('tensor', 'dp')
- grad_b_down: float32 [768], P('dp')
- grad_g_three: float32 [768], P('dp')
- grad_c_three: float32 [768], P('dp')
The draws below stay inside these ranges and needn't reach their ends.
Inputs may be any that keep to these rules, and one draw needn't show every extreme that they name: `lengths`: some sequence has exactly 512 live tokens. The 1024 indices of one query are distinct.
All inputs are finite; a program needn't handle non-finite values.
Results may differ from the reference program's by a relative error of at most 0.025.
Values sent between devices are 32-bit elements; how exact they have to be, the bound alone decides.
No kernel may reach another device: no remote copies, remote signals or barrier semaphores. Data moves between devices by JAX's collectives and lax.ppermute only.
A program may use at most 192 MiB of HBM per device.

```python
import math
import jax
import jax.numpy as jnp
from jax import lax

D = 768
H = 12
HD = 64
FF = 3072
LEN = 512
DS = 2048
K = 1024
SEQS = 16


def draw_lengths(key, part):
    key = jax.random.fold_in(key, 11)
    key_values, key_longest = jax.random.split(key)
    values = jax.random.randint(key_values, (SEQS,), LEN // 8, LEN + 1)
    longest = jax.random.randint(key_longest, (), 0, SEQS)
    return jnp.where(jnp.arange(SEQS) == longest, LEN, values).astype(jnp.int32)


def draw_indices(key, part):
    key = jax.random.fold_in(key, 23)
    row_keys = jax.random.split(key, SEQS * LEN)
    picked = jax.vmap(lambda single_key: jax.random.permutation(single_key, DS)[:K])(row_keys)
    return picked.reshape(SEQS, LEN, K).astype(jnp.int32)


def with_spikes(drawn, key, source, target, blocks, factor):
    def block_of(dim):
        return (jnp.arange(drawn.shape[dim]) // (drawn.shape[dim] // blocks)).reshape((-1,) + (1,) * (drawn.ndim - 1 - dim))

    first = jax.random.permutation(key, blocks)[block_of(target)]
    second = (block_of(target) + blocks // 2) % blocks
    return jnp.where((block_of(source) == first) | (block_of(source) == second), factor * drawn, drawn)


def steps_of(rng, dims, cuts, smallest, high):
    level, own = 1.0, jax.random.fold_in(rng, 6)
    for dim, shards_of in cuts:
        steps = jnp.exp(jax.random.uniform(jax.random.fold_in(own, dim), (shards_of,), jnp.float32, smallest / len(cuts), high / len(cuts)))
        level = level * jnp.repeat(steps, dims[dim] // shards_of).reshape([-1 if axis == dim else 1 for axis in range(len(dims))])
    return level


def bell_draw(key, extent, scale, most, pieces=(), kind=jnp.bfloat16):
    values = jax.random.normal(key, extent, jnp.float32) * scale
    if len(pieces) > 0:
        values = steps_of(key, extent, pieces, -0.22, 0.18) * values
    return jnp.clip(values, min=-most, max=most).astype(kind)


def gaussian_with(rng, extent, width, reach, shards, heavy, kind=jnp.bfloat16):
    values = width * jax.random.normal(rng, extent, jnp.float32)
    if shards:
        values = values * steps_of(rng, extent, shards, -0.22, 0.18)
    return jnp.clip(with_spikes(values, jax.random.fold_in(rng, 3), *heavy), -reach, reach).astype(kind)


def setup_inputs(seed: int = 0) -> dict:
    key_of = jax.random.split(jax.random.key(seed), 30)
    return {
        "inputs": gaussian_with(key_of[0], (SEQS, LEN, D), 1.0, 6.0, ((0, 16),), (0, 2, 16, 2.0)),
        "datastore": bell_draw(key_of[1], (SEQS, DS, D), 1.0, 6.0, ((0, 16),)),
        "lengths": draw_lengths(jax.random.fold_in(key_of[29], 71), 0),
        "indices": draw_indices(jax.random.fold_in(key_of[29], 71), 0),
        "w_query": bell_draw(key_of[4], (D, H * HD), D ** -0.5, 0.21875, ((1, 2),)),
        "b_query": bell_draw(key_of[5], (H * HD,), 0.3, 2.0, ((0, 2),)),
        "w_key": bell_draw(key_of[6], (D, H * HD), D ** -0.5, 0.21875, ((1, 2),)),
        "w_value": bell_draw(key_of[7], (D, H * HD), D ** -0.5, 0.21875, ((1, 2),)),
        "b_value": bell_draw(key_of[8], (H * HD,), 0.08, 0.5, ((0, 2),)),
        "w_out": bell_draw(key_of[9], (H * HD, D), (max(1, H * HD * 4 // LEN)) ** -0.5, 2.5, ((0, 2),)),
        "b_out": bell_draw(key_of[10], (D,), 0.3, 2.0),
        "g_one": jnp.clip(1.0 + 0.1 * jax.random.normal(key_of[11], (D,), jnp.float32), 0.5, 1.5).astype(jnp.bfloat16),
        "c_one": bell_draw(key_of[12], (D,), 0.3, 2.0),
        "wc_query": bell_draw(key_of[13], (D, H * HD), D ** -0.5, 0.21875, ((1, 2),)),
        "bc_query": bell_draw(key_of[14], (H * HD,), 0.3, 2.0, ((0, 2),)),
        "wc_key": bell_draw(key_of[15], (D, H * HD), D ** -0.5, 0.21875, ((1, 2),)),
        "wc_value": bell_draw(key_of[16], (D, H * HD), D ** -0.5, 0.21875, ((1, 2),)),
        "bc_value": bell_draw(key_of[17], (H * HD,), 0.08, 0.5, ((0, 2),)),
        "wc_out": bell_draw(key_of[18], (H * HD, D), (max(1, H * HD * 4 // K)) ** -0.5, 3.5, ((0, 2),)),
        "bc_out": bell_draw(key_of[19], (D,), 0.3, 2.0),
        "g_two": jnp.clip(1.0 + 0.1 * jax.random.normal(key_of[20], (D,), jnp.float32), 0.5, 1.5).astype(jnp.bfloat16),
        "c_two": bell_draw(key_of[21], (D,), 0.3, 2.0),
        "w_up": bell_draw(key_of[22], (D, FF), D ** -0.5, 0.21875, ((1, 2),)),
        "b_up": bell_draw(key_of[23], (FF,), 0.5, 3.0, ((0, 2),)),
        "w_down": bell_draw(key_of[24], (FF, D), (FF // 4) ** -0.5, 0.21875, ((0, 2),)),
        "b_down": bell_draw(key_of[25], (D,), 0.3, 2.0),
        "g_three": jnp.clip(1.0 + 0.1 * jax.random.normal(key_of[26], (D,), jnp.float32), 0.5, 1.5).astype(jnp.bfloat16),
        "c_three": bell_draw(key_of[27], (D,), 0.3, 2.0),
        "cotangent": gaussian_with(key_of[28], (SEQS, LEN, D), 1.0, 6.0, ((0, 16),), (0, 2, 16, 2.0)),
    }


HIGHEST = lax.Precision.HIGHEST
NEG = -1e+30

@jax.custom_vjp
def low(v):
    return lax.optimization_barrier(v.astype(jnp.bfloat16)).astype(jnp.float32)

@jax.custom_vjp
def low_back(v):
    return v

def low_keep(v):
    return (low(v), None)

def low_pass(kept, grad):
    return (grad,)

def back_keep(v):
    return (v, None)

def back_low(kept, grad):
    return (low(grad),)
low.defvjp(low_keep, low_pass)
low_back.defvjp(back_keep, back_low)

def contract(form, left, right):
    return jnp.einsum(form, left, right, precision=HIGHEST)

def layer_norm(values, gain, shift):
    average = lax.optimization_barrier(jnp.mean(values, axis=-1, keepdims=True))
    centred = values - average
    variance = lax.optimization_barrier(jnp.mean(centred * centred, axis=-1, keepdims=True))
    return centred * lax.rsqrt(variance + 1e-05) * gain + shift

def layer(params, inputs, memory, length, picks):
    w_query, b_query, w_key, w_value, b_value, w_out, b_out, g_one, c_one, wc_query, bc_query, wc_key, wc_value, bc_value, wc_out, bc_out, g_two, c_two, w_up, b_up, w_down, b_down, g_three, c_three = params
    seq_rows = inputs.shape[0]
    q_scale = 1.0 / math.sqrt(HD)
    position = jnp.arange(seq_rows)
    queries = low_back(low((contract('rd,dc->rc', inputs, w_query) + b_query) * q_scale)).reshape(seq_rows, H, HD)
    keys_self = low_back(low(contract('rd,dc->rc', inputs, w_key))).reshape(seq_rows, H, HD)
    values_self = low_back(low(contract('rd,dc->rc', inputs, w_value) + b_value)).reshape(seq_rows, H, HD)
    allowed = (position[None, :] <= position[:, None]) & (position[None, :] < length)
    scores = low_back(contract('qhe,khe->hqk', queries, keys_self))
    self_probs = low(jax.nn.softmax(jnp.where(allowed[None], scores, NEG), axis=-1))
    attended = low_back(low(contract('hqk,khe->qhe', self_probs, values_self))).reshape(seq_rows, H * HD)
    self_out = low_back(contract('rc,cd->rd', attended, w_out) + b_out)
    normed_one = layer_norm(inputs + self_out, g_one, c_one)
    cross_query = low_back(low((contract('rd,dc->rc', low(normed_one), wc_query) + bc_query) * q_scale)).reshape(seq_rows, H, HD)
    projected = low_back(low(contract('qhe,dhe->qhd', cross_query, wc_key.reshape(D, H, HD))))
    chosen = jnp.zeros((seq_rows, DS), dtype=jnp.bool_).at[position[:, None], picks].set(True)
    cross_scores = low_back(contract('qhd,md->hqm', projected, memory))
    cross_probs = low(jax.nn.softmax(jnp.where(chosen[None], cross_scores, NEG), axis=-1))
    pooled = low_back(low(contract('hqm,md->qhd', cross_probs, memory)))
    context = low_back(low(contract('qhd,dhe->qhe', pooled, wc_value.reshape(D, H, HD)) + bc_value.reshape(H, HD))).reshape(seq_rows, H * HD)
    cross_out = low_back(contract('rc,cd->rd', context, wc_out) + bc_out)
    normed_two = layer_norm(normed_one + cross_out, g_two, c_two)
    pre_act = low_back(contract('rd,df->rf', low(normed_two), w_up) + b_up)
    hidden = low(jax.nn.gelu(pre_act, approximate=False))
    ffn_out = low_back(contract('rf,fd->rd', hidden, w_down) + b_down)
    return layer_norm(normed_two + ffn_out, g_three, c_three)

def reference(inputs, datastore, lengths, indices, w_query, b_query, w_key, w_value, b_value, w_out, b_out, g_one, c_one, wc_query, bc_query, wc_key, wc_value, bc_value, wc_out, bc_out, g_two, c_two, w_up, b_up, w_down, b_down, g_three, c_three, cotangent):
    params = tuple((weight.astype(jnp.float32) for weight in (w_query, b_query, w_key, w_value, b_value, w_out, b_out, g_one, c_one, wc_query, bc_query, wc_key, wc_value, bc_value, wc_out, bc_out, g_two, c_two, w_up, b_up, w_down, b_down, g_three, c_three)))

    def one_sequence(totals, sample):
        values, memory, length, picks, seed_grad = sample

        def forward_fn(weights, rows_in, store_in):
            return layer(weights, rows_in, store_in, length, picks.astype(jnp.int32))
        result, pullback = jax.vjp(forward_fn, params, values.astype(jnp.float32), memory.astype(jnp.float32))
        weight_grads, row_grads, store_grads = pullback(seed_grad.astype(jnp.float32))
        totals = jax.tree.map(jnp.add, totals, weight_grads)
        return (totals, (result.astype(jnp.bfloat16), row_grads, store_grads))
    initial = jax.tree.map(jnp.zeros_like, params)
    totals, (outputs, input_grads, store_grads) = lax.scan(one_sequence, initial, (inputs, datastore, lengths, indices, cotangent))
    return (outputs, input_grads, store_grads, totals[0], totals[1], totals[2], totals[3], totals[4], totals[5], totals[6], totals[7], totals[8], totals[9], totals[10], totals[11], totals[12], totals[13], totals[14], totals[15], totals[16], totals[17], totals[18], totals[19], totals[20], totals[21], totals[22], totals[23])
```

```python
import functools
import math

import jax
import jax.numpy as jnp
from jax import lax
from jax.experimental import pallas as pl
from jax.experimental.pallas import tpu as pltpu
from jax.sharding import PartitionSpec as P

HD = 64
NEG = -1e30
EPS = 1e-05
WORDS = 256
MIB = 1 << 20

F32 = jnp.float32
LOW = jnp.bfloat16


def nn(left, right):
    return lax.dot_general(left, right, (((1,), (0,)), ((), ())), preferred_element_type=F32)


def nt(left, right):
    return lax.dot_general(left, right, (((1,), (1,)), ((), ())), preferred_element_type=F32)


def tn(left, right):
    return lax.dot_general(left, right, (((0,), (0,)), ((), ())), preferred_element_type=F32)


def flip(values):
    return values.astype(F32).T


def vmem():
    return pl.BlockSpec(memory_space=pltpu.VMEM)


def smem():
    return pl.BlockSpec(memory_space=pltpu.SMEM)


def shape(dims, kind=F32):
    return jax.ShapeDtypeStruct(dims, kind)


def cost(micros):
    return pl.CostEstimate(flops=int(micros * 6e8), bytes_accessed=1, transcendentals=0)


def params(mib, grid=None):
    kinds = None if grid is None else ("arbitrary",) * grid
    return pltpu.CompilerParams(vmem_limit_bytes=mib * MIB, dimension_semantics=kinds)


def norm_parts(values):
    average = jnp.mean(values, axis=-1, keepdims=True)
    centred = values - average
    variance = jnp.mean(centred * centred, axis=-1, keepdims=True)
    inverse = lax.rsqrt(variance + EPS)
    return centred * inverse, inverse


def norm_back(grad, gain, unit, inverse):
    scaled = grad * gain
    first = jnp.mean(scaled, axis=-1, keepdims=True)
    second = jnp.mean(scaled * unit, axis=-1, keepdims=True)
    return inverse * (scaled - first - unit * second)


def rows_of_half(values, half):
    row = lax.broadcasted_iota(jnp.int32, values.shape, 0)
    return jnp.where((row // HD) == half, values, jnp.zeros_like(values))


def lanes_of_half(values, half):
    lane = lax.broadcasted_iota(jnp.int32, values.shape, 1)
    return jnp.where((lane // HD) == half, values, jnp.zeros_like(values))


def self_forward_body(
    length, x, wq, bq, wk, wv, bv, wo, q_out, k_out, v_out, p_out, inv_out, ot_out, att_out, part_out, bias
):
    rows = x.shape[0]
    heads = wq.shape[1] // HD
    q_scale = 1.0 / math.sqrt(HD)
    x_low = x[...]
    q = ((nn(x_low, wq[...]) + bq[...]) * q_scale).astype(LOW)
    k = nn(x_low, wk[...]).astype(LOW)
    v = (nn(x_low, wv[...]) + bv[...]).astype(LOW)
    q_out[...] = q
    k_out[...] = k
    v_out[...] = v
    qt = flip(q).astype(LOW)
    vt = flip(v).astype(LOW)
    key = lax.broadcasted_iota(jnp.int32, (rows, rows), 0)
    query = lax.broadcasted_iota(jnp.int32, (rows, rows), 1)
    bias[...] = jnp.where((key <= query) & (key < length[0]), 0.0, NEG)
    for head in range(heads):
        pair, half = head // 2, head % 2
        lanes = slice(pair * 2 * HD, (pair + 1) * 2 * HD)
        own = slice(head * HD, (head + 1) * HD)
        scores = nn(k[:, lanes], rows_of_half(qt[lanes], half)) + bias[...]
        top = jnp.max(scores, axis=0, keepdims=True)
        grown = jnp.exp(scores - top)
        inverse = 1.0 / jnp.sum(grown, axis=0, keepdims=True)
        low = grown.astype(LOW)
        p_out[head] = low
        inv_out[pl.ds(head, 1), :] = inverse
        ot_out[own, :] = nn(vt[own], low) * inverse
    attended = ot_out[...].T.astype(LOW)
    att_out[...] = attended
    part_out[...] = nn(attended, wo[...])


def self_forward(length, x, wq, bq, wk, wv, bv, wo):
    rows, width = x.shape
    cols = wq.shape[1]
    heads = cols // HD
    return pl.pallas_call(
        self_forward_body,
        out_shape=(
            shape((rows, cols), LOW),
            shape((rows, cols), LOW),
            shape((rows, cols), LOW),
            shape((heads, rows, rows), LOW),
            shape((heads, rows)),
            shape((cols, rows)),
            shape((rows, cols), LOW),
            shape((rows, width)),
        ),
        in_specs=[smem()] + [vmem()] * 7,
        out_specs=(vmem(),) * 8,
        scratch_shapes=[pltpu.VMEM((rows, rows), F32)],
        compiler_params=params(32),
        cost_estimate=cost(10),
        name="self_forward",
    )(length, x, wq, bq, wk, wv, bv, wo)


def mask_body(picks, words, sums):
    step = pl.program_id(0)
    block = picks.shape[0]
    row = lax.broadcasted_iota(jnp.int32, (256, 256), 0)
    col = lax.broadcasted_iota(jnp.int32, (256, 256), 1)
    same = (row & 15) == (col & 15)
    for part in range(block // 16):
        index = picks[part * 16 : (part + 1) * 16, :]
        bit = lax.shift_left(jnp.ones_like(index), index >> 8).astype(F32).astype(LOW)
        upper = ((index >> 4) & 15).astype(F32).astype(LOW)
        lower = (index & 15).astype(F32).astype(LOW)
        zero = jnp.zeros_like(bit)
        one = jnp.ones_like(bit)
        left = jnp.concatenate([jnp.where(upper == c, bit, zero) for c in range(16)], axis=0)
        right = jnp.concatenate([jnp.where(lower == c, one, zero) for c in range(16)], axis=0)
        cross = jnp.where(same, nt(left, right), 0.0).astype(LOW)
        start = pl.multiple_of(step * block + part * 16, 16)
        for c in range(16):
            sums[pl.ds(start, 16), c * 256 : (c + 1) * 256] = cross[c * 16 : (c + 1) * 16, :]

    @pl.when(step == pl.num_programs(0) - 1)
    def _():
        word = lax.broadcasted_iota(jnp.int32, (256, 4096), 0)
        place = lax.broadcasted_iota(jnp.int32, (256, 4096), 1)
        fold = jnp.where((place >> 4) == word, 1.0, 0.0).astype(LOW)
        words[...] = nt(fold, sums[...]).astype(jnp.int32)


def mask_words(picks):
    rows, chosen = picks.shape
    block = math.gcd(rows, 64)
    return pl.pallas_call(
        mask_body,
        grid=(rows // block,),
        out_shape=shape((WORDS, rows), jnp.int32),
        in_specs=[pl.BlockSpec((block, chosen), lambda i: (i, 0))],
        out_specs=pl.BlockSpec((WORDS, rows), lambda i: (0, 0)),
        scratch_shapes=[pltpu.VMEM((rows, 16 * 256), LOW)],
        compiler_params=params(32, 1),
        cost_estimate=cost(10),
        name="mask_words",
    )(picks)


def store_body(memory, wk, wv, k_out, v_out, kt_out, vt_out):
    low = memory[...]
    k_out[...] = nn(low, wk[...]).astype(LOW)
    v_out[...] = nn(low, wv[...]).astype(LOW)
    kt_out[...] = lax.dot_general(
        wk[...], low, (((0,), (1,)), ((), ())), preferred_element_type=F32
    ).astype(LOW)
    vt_out[...] = lax.dot_general(
        wv[...], low, (((0,), (1,)), ((), ())), preferred_element_type=F32
    ).astype(LOW)


def store_products(memory, wk, wv):
    entries, width = memory.shape
    cols = wk.shape[1]
    block = 512
    return pl.pallas_call(
        store_body,
        grid=(entries // block,),
        out_shape=(
            shape((entries, cols), LOW),
            shape((entries, cols), LOW),
            shape((cols, entries), LOW),
            shape((cols, entries), LOW),
        ),
        in_specs=[
            pl.BlockSpec((block, width), lambda i: (i, 0)),
            pl.BlockSpec((width, cols), lambda i: (0, 0)),
            pl.BlockSpec((width, cols), lambda i: (0, 0)),
        ],
        out_specs=(
            pl.BlockSpec((block, cols), lambda i: (i, 0)),
            pl.BlockSpec((block, cols), lambda i: (i, 0)),
            pl.BlockSpec((cols, block), lambda i: (0, i)),
            pl.BlockSpec((cols, block), lambda i: (0, i)),
        ),
        compiler_params=params(32, 1),
        cost_estimate=cost(8),
        name="store_products",
    )(memory, wk, wv)


def cross_forward_body(
    x, own, other, b_out, g_one, c_one, wq, bq, words, keys, values_t, bv, wo,
    unit_out, inv_out, low_out, q_out, p_out, sum_out, ot_out, ctx_out, part_out,
    qt, bias, scores, ctx_t,
):
    step = pl.program_id(0)
    q_scale = 1.0 / math.sqrt(HD)
    entries = keys.shape[0]
    chunk = WORDS

    @pl.when(step == 0)
    def _():
        total = x[...].astype(F32) + (own[...] + other[...] + b_out[...])
        unit, inverse = norm_parts(total)
        unit_out[...] = unit
        inv_out[...] = inverse
        low = (unit * g_one[...] + c_one[...]).astype(LOW)
        low_out[...] = low
        q = ((nn(low, wq[...]) + bq[...]) * q_scale).astype(LOW)
        q_out[...] = q
        qt[...] = flip(q).astype(LOW)
        held = words[...]
        for part in range(entries // chunk):
            bias[part * chunk : (part + 1) * chunk, :] = jnp.where(((held >> part) & 1) == 1, 0.0, NEG)

    pair_rows = qt[pl.ds(pl.multiple_of(step * 2 * HD, 2 * HD), 2 * HD), :]
    for half in range(2):
        query = rows_of_half(pair_rows, half)
        top = None
        for part in range(entries // chunk):
            span = slice(part * chunk, (part + 1) * chunk)
            piece = nn(keys[span, :], query) + bias[span, :]
            scores[half, span, :] = piece
            peak = jnp.max(piece, axis=0, keepdims=True)
            top = peak if top is None else jnp.maximum(top, peak)
        total = None
        for part in range(entries // chunk):
            span = slice(part * chunk, (part + 1) * chunk)
            grown = jnp.exp(scores[half, span, :] - top)
            p_out[half, span, :] = grown.astype(LOW)
            mass = jnp.sum(grown, axis=0, keepdims=True)
            total = mass if total is None else total + mass
        inverse = 1.0 / total
        sum_out[0, pl.ds(half, 1), :] = inverse
        pooled = nn(values_t[half * HD : (half + 1) * HD, :], p_out[half]) * inverse
        ot_out[half * HD : (half + 1) * HD, :] = pooled
        ctx_t[pl.ds(pl.multiple_of(step * 2 * HD + half * HD, HD), HD), :] = pooled

    @pl.when(step == pl.num_programs(0) - 1)
    def _():
        context = (ctx_t[...].T + bv[...]).astype(LOW)
        ctx_out[...] = context
        part_out[...] = nn(context, wo[...])


def cross_forward(x, own, other, b_out, g_one, c_one, wq, bq, words, keys, values_t, bv, wo):
    rows, width = x.shape
    entries, cols = keys.shape
    pairs = cols // (2 * HD)

    def whole(dims):
        return pl.BlockSpec(dims, lambda i: (0,) * len(dims))

    return pl.pallas_call(
        cross_forward_body,
        grid=(pairs,),
        out_shape=(
            shape((rows, width)),
            shape((rows, 1)),
            shape((rows, width), LOW),
            shape((rows, cols), LOW),
            shape((2 * pairs, entries, rows), LOW),
            shape((pairs, 2, rows)),
            shape((cols, rows)),
            shape((rows, cols), LOW),
            shape((rows, width)),
        ),
        in_specs=[
            whole((rows, width)),
            whole((rows, width)),
            whole((rows, width)),
            whole((1, width)),
            whole((1, width)),
            whole((1, width)),
            whole((width, cols)),
            whole((1, cols)),
            whole((WORDS, rows)),
            pl.BlockSpec((entries, 2 * HD), lambda i: (0, i)),
            pl.BlockSpec((2 * HD, entries), lambda i: (i, 0)),
            whole((1, cols)),
            whole((cols, width)),
        ],
        out_specs=(
            whole((rows, width)),
            whole((rows, 1)),
            whole((rows, width)),
            whole((rows, cols)),
            pl.BlockSpec((2, entries, rows), lambda i: (i, 0, 0)),
            pl.BlockSpec((1, 2, rows), lambda i: (i, 0, 0)),
            pl.BlockSpec((2 * HD, rows), lambda i: (i, 0)),
            whole((rows, cols)),
            whole((rows, width)),
        ),
        scratch_shapes=[
            pltpu.VMEM((cols, rows), LOW),
            pltpu.VMEM((entries, rows), F32),
            pltpu.VMEM((2, entries, rows), F32),
            pltpu.VMEM((cols, rows), F32),
        ],
        compiler_params=params(56, 1),
        cost_estimate=cost(16),
        name="cross_forward",
    )(x, own, other, b_out, g_one, c_one, wq, bq, words, keys, values_t, bv, wo)


def ffn_forward_body(
    unit_one, g_one, c_one, own, other, b_out, g_two, c_two, w_up, b_up, w_down,
    unit_out, inv_out, low_out, hid_out, slope_out, part_out,
):
    step = pl.program_id(0)

    @pl.when(step == 0)
    def _():
        total = unit_one[...] * g_one[...] + c_one[...] + (own[...] + other[...] + b_out[...])
        unit, inverse = norm_parts(total)
        unit_out[...] = unit
        inv_out[...] = inverse
        low_out[...] = (unit * g_two[...] + c_two[...]).astype(LOW)

    pre = nn(low_out[...], w_up[...]) + b_up[...]
    below = 0.5 * (1.0 + lax.erf(pre * math.sqrt(0.5)))
    density = jnp.exp(-0.5 * pre * pre) * (1.0 / math.sqrt(2.0 * math.pi))
    slope_out[...] = below + pre * density
    hidden = (pre * below).astype(LOW)
    hid_out[...] = hidden
    term = nn(hidden, w_down[...])

    @pl.when(step == 0)
    def _():
        part_out[...] = term

    @pl.when(step > 0)
    def _():
        part_out[...] += term


def ffn_forward(unit_one, g_one, c_one, own, other, b_out, g_two, c_two, w_up, b_up, w_down):
    rows, width = unit_one.shape
    units = w_up.shape[1]
    block = 512

    def whole(dims):
        return pl.BlockSpec(dims, lambda i: (0,) * len(dims))

    return pl.pallas_call(
        ffn_forward_body,
        grid=(units // block,),
        out_shape=(
            shape((rows, width)),
            shape((rows, 1)),
            shape((rows, width), LOW),
            shape((rows, units), LOW),
            shape((rows, units)),
            shape((rows, width)),
        ),
        in_specs=[
            whole((rows, width)),
            whole((1, width)),
            whole((1, width)),
            whole((rows, width)),
            whole((rows, width)),
            whole((1, width)),
            whole((1, width)),
            whole((1, width)),
            pl.BlockSpec((width, block), lambda i: (0, i)),
            pl.BlockSpec((1, block), lambda i: (0, i)),
            pl.BlockSpec((block, width), lambda i: (i, 0)),
        ],
        out_specs=(
            whole((rows, width)),
            whole((rows, 1)),
            whole((rows, width)),
            pl.BlockSpec((rows, block), lambda i: (0, i)),
            pl.BlockSpec((rows, block), lambda i: (0, i)),
            whole((rows, width)),
        ),
        compiler_params=params(40, 1),
        cost_estimate=cost(8),
        name="ffn_forward",
    )(unit_one, g_one, c_one, own, other, b_out, g_two, c_two, w_up, b_up, w_down)


def norm_three_body(unit_two, g_two, c_two, own, other, b_down, g_three, c_three, cotangent, out, grad, low, sums):
    total = unit_two[...] * g_two[...] + c_two[...] + (own[...] + other[...] + b_down[...])
    unit, inverse = norm_parts(total)
    out[...] = (unit * g_three[...] + c_three[...]).astype(LOW)
    seed = cotangent[...].astype(F32)
    back = norm_back(seed, g_three[...], unit, inverse)
    rounded = back.astype(LOW)
    grad[...] = back
    low[...] = rounded
    sums[0:1, :] = jnp.sum(seed * unit, axis=0, keepdims=True)
    sums[1:2, :] = jnp.sum(seed, axis=0, keepdims=True)
    sums[2:3, :] = jnp.sum(rounded.astype(F32), axis=0, keepdims=True)


def norm_three(unit_two, g_two, c_two, own, other, b_down, g_three, c_three, cotangent):
    rows, width = unit_two.shape
    return pl.pallas_call(
        norm_three_body,
        out_shape=(shape((rows, width), LOW), shape((rows, width)), shape((rows, width), LOW), shape((3, width))),
        in_specs=[vmem()] * 9,
        out_specs=(vmem(),) * 4,
        compiler_params=params(24),
        cost_estimate=cost(3),
        name="norm_three",
    )(unit_two, g_two, c_two, own, other, b_down, g_three, c_three, cotangent)


def cross_backward_body(
    grad_three, own, other, unit_two, inv_two, g_two, wo, ot, sums, probs, values, keys_t, query, wq,
    grad_out, low_out, norm_sums, head_sums, dk_out, dv_out, dq_out, part_out,
    dctx_t, dq_t, change,
):
    step = pl.program_id(0)
    q_scale = 1.0 / math.sqrt(HD)
    entries = values.shape[0]
    chunk = WORDS

    @pl.when(step == 0)
    def _():
        grad_in = grad_three[...] + (own[...] + other[...])
        unit = unit_two[...]
        grad = norm_back(grad_in, g_two[...], unit, inv_two[...])
        grad_out[...] = grad
        low = grad.astype(LOW)
        low_out[...] = low
        norm_sums[0:1, :] = jnp.sum(grad_in * unit, axis=0, keepdims=True)
        norm_sums[1:2, :] = jnp.sum(grad_in, axis=0, keepdims=True)
        norm_sums[2:3, :] = jnp.sum(low.astype(F32), axis=0, keepdims=True)
        dctx_t[...] = nt(wo[...], low)
        head_sums[0:1, :] = jnp.sum(dctx_t[...].T, axis=0, keepdims=True)

    pair_start = pl.multiple_of(step * 2 * HD, 2 * HD)
    pair_grad = dctx_t[pl.ds(pair_start, 2 * HD), :]
    row = lax.broadcasted_iota(jnp.int32, pair_grad.shape, 0)
    scaled = pair_grad * jnp.where(row < HD, sums[0, 0:1, :], sums[0, 1:2, :])
    scaled_low = scaled.astype(LOW)
    weighed = scaled_low.astype(F32) * ot[...]
    scaled_rows = flip(scaled_low).astype(LOW)
    pair_query = query[...]
    for half in range(2):
        inner = jnp.sum(weighed[half * HD : (half + 1) * HD, :], axis=0, keepdims=True)
        grad_rows = rows_of_half(scaled_low, half)
        own_query = lanes_of_half(pair_query, half)
        own_grad = lanes_of_half(scaled_rows, half)
        for part in range(entries // chunk):
            span = slice(part * chunk, (part + 1) * chunk)
            low_probs = probs[half, span, :]
            shift = nn(values[span, :], grad_rows) - inner
            delta = (low_probs.astype(F32) * shift).astype(LOW)
            change[span, :] = delta
            k_term = nn(delta, own_query)
            v_term = nn(low_probs, own_grad)
            if half == 0:
                dk_out[span, :] = k_term.astype(LOW)
                dv_out[span, :] = v_term.astype(LOW)
            else:
                dk_out[span, :] = dk_out[span, :] + k_term.astype(LOW)
                dv_out[span, :] = dv_out[span, :] + v_term.astype(LOW)
        start = pl.multiple_of(step * 2 * HD + half * HD, HD)
        dq_t[pl.ds(start, HD), :] = nn(keys_t[half * HD : (half + 1) * HD, :], change[...])

    @pl.when(step == pl.num_programs(0) - 1)
    def _():
        dq = dq_t[...].T.astype(LOW)
        dq_out[...] = dq
        head_sums[1:2, :] = jnp.sum(dq.astype(F32), axis=0, keepdims=True) * q_scale
        part_out[...] = nt(dq, wq[...]) * q_scale


def cross_backward(grad_three, own, other, unit_two, inv_two, g_two, wo, ot, sums, probs, values, keys_t, query, wq):
    rows, width = grad_three.shape
    entries, cols = values.shape
    pairs = cols // (2 * HD)

    def whole(dims):
        return pl.BlockSpec(dims, lambda i: (0,) * len(dims))

    return pl.pallas_call(
        cross_backward_body,
        grid=(pairs,),
        out_shape=(
            shape((rows, width)),
            shape((rows, width), LOW),
            shape((3, width)),
            shape((2, cols)),
            shape((entries, cols), LOW),
            shape((entries, cols), LOW),
            shape((rows, cols), LOW),
            shape((rows, width)),
        ),
        in_specs=[
            whole((rows, width)),
            whole((rows, width)),
            whole((rows, width)),
            whole((rows, width)),
            whole((rows, 1)),
            whole((1, width)),
            whole((cols, width)),
            pl.BlockSpec((2 * HD, rows), lambda i: (i, 0)),
            pl.BlockSpec((1, 2, rows), lambda i: (i, 0, 0)),
            pl.BlockSpec((2, entries, rows), lambda i: (i, 0, 0)),
            pl.BlockSpec((entries, 2 * HD), lambda i: (0, i)),
            pl.BlockSpec((2 * HD, entries), lambda i: (i, 0)),
            pl.BlockSpec((rows, 2 * HD), lambda i: (0, i)),
            whole((width, cols)),
        ],
        out_specs=(
            whole((rows, width)),
            whole((rows, width)),
            whole((3, width)),
            whole((2, cols)),
            pl.BlockSpec((entries, 2 * HD), lambda i: (0, i)),
            pl.BlockSpec((entries, 2 * HD), lambda i: (0, i)),
            whole((rows, cols)),
            whole((rows, width)),
        ),
        scratch_shapes=[
            pltpu.VMEM((cols, rows), F32),
            pltpu.VMEM((cols, rows), F32),
            pltpu.VMEM((entries, rows), LOW),
        ],
        compiler_params=params(56, 1),
        cost_estimate=cost(22),
        name="cross_backward",
    )(grad_three, own, other, unit_two, inv_two, g_two, wo, ot, sums, probs, values, keys_t, query, wq)


def self_backward_body(
    grad_two, own, other, unit_one, inv_one, g_one, wo, ot, inverse, probs, q, k, v, wq, wk, wv,
    grad_out, low_out, norm_sums, head_sums, dq_out, dk_out, dv_out, part_out,
    dq_t,
):
    q_scale = 1.0 / math.sqrt(HD)
    heads = q.shape[1] // HD
    grad_in = grad_two[...] + (own[...] + other[...])
    unit = unit_one[...]
    grad = norm_back(grad_in, g_one[...], unit, inv_one[...])
    grad_out[...] = grad
    low = grad.astype(LOW)
    low_out[...] = low
    norm_sums[0:1, :] = jnp.sum(grad_in * unit, axis=0, keepdims=True)
    norm_sums[1:2, :] = jnp.sum(grad_in, axis=0, keepdims=True)
    norm_sums[2:3, :] = jnp.sum(low.astype(F32), axis=0, keepdims=True)
    datt_t = nt(wo[...], low)
    keys_t = flip(k[...]).astype(LOW)
    for pair in range(heads // 2):
        lanes = slice(pair * 2 * HD, (pair + 1) * 2 * HD)
        pair_grad = datt_t[lanes]
        row = lax.broadcasted_iota(jnp.int32, pair_grad.shape, 0)
        scaled = pair_grad * jnp.where(
            row < HD, inverse[2 * pair : 2 * pair + 1, :], inverse[2 * pair + 1 : 2 * pair + 2, :]
        )
        scaled_low = scaled.astype(LOW)
        weighed = scaled_low.astype(F32) * ot[lanes, :]
        scaled_rows = flip(scaled_low).astype(LOW)
        pair_query = q[:, lanes]
        pair_values = v[:, lanes]
        dk = None
        dv = None
        for half in range(2):
            head = 2 * pair + half
            inner = jnp.sum(weighed[half * HD : (half + 1) * HD, :], axis=0, keepdims=True)
            low_probs = probs[head]
            shift = nn(pair_values, rows_of_half(scaled_low, half)) - inner
            delta = (low_probs.astype(F32) * shift).astype(LOW)
            k_term = nn(delta, lanes_of_half(pair_query, half))
            v_term = nn(low_probs, lanes_of_half(scaled_rows, half))
            dk = k_term if dk is None else dk + k_term
            dv = v_term if dv is None else dv + v_term
            own_rows = slice(head * HD, (head + 1) * HD)
            dq_t[own_rows, :] = nn(keys_t[own_rows], delta)
        dk_out[:, lanes] = dk.astype(LOW)
        dv_out[:, lanes] = dv.astype(LOW)
    dq = dq_t[...].T.astype(LOW)
    dq_out[...] = dq
    head_sums[0:1, :] = jnp.sum(dq.astype(F32), axis=0, keepdims=True) * q_scale
    head_sums[1:2, :] = jnp.sum(dv_out[...].astype(F32), axis=0, keepdims=True)
    part_out[...] = nt(dq, wq[...]) * q_scale + nt(dk_out[...], wk[...]) + nt(dv_out[...], wv[...])


def self_backward(grad_two, own, other, unit_one, inv_one, g_one, wo, ot, inverse, probs, q, k, v, wq, wk, wv):
    rows, width = grad_two.shape
    cols = q.shape[1]
    return pl.pallas_call(
        self_backward_body,
        out_shape=(
            shape((rows, width)),
            shape((rows, width), LOW),
            shape((3, width)),
            shape((2, cols)),
            shape((rows, cols), LOW),
            shape((rows, cols), LOW),
            shape((rows, cols), LOW),
            shape((rows, width)),
        ),
        in_specs=[vmem()] * 16,
        out_specs=(vmem(),) * 8,
        scratch_shapes=[pltpu.VMEM((cols, rows), F32)],
        compiler_params=params(40),
        cost_estimate=cost(12),
        name="self_backward",
    )(grad_two, own, other, unit_one, inv_one, g_one, wo, ot, inverse, probs, q, k, v, wq, wk, wv)


def block_order(bits):
    count = len(bits)
    return [
        sum((1 - ((place >> (count - 1 - i)) & 1)) << bit for i, bit in enumerate(bits))
        for place in range(1 << count)
    ]


def spread_body(own, values, out, turned, *, order):
    size = out.shape[0] // len(order)
    turned[...] = flip(values[...]).astype(LOW)
    for place, offset in enumerate(order):
        source = pl.multiple_of((own[0] ^ offset) * size, 16)
        out[place * size : (place + 1) * size, :] = turned[pl.ds(source, size), :]


def turn_body(values, out):
    out[...] = flip(values[...]).astype(LOW)


def spread(own, values, bits):
    rows, width = values.shape
    order = block_order(bits)
    size = width // len(order)
    mib = 4 + (rows * width * 12) // MIB
    if size % 16 == 0:
        return pl.pallas_call(
            functools.partial(spread_body, order=order),
            out_shape=shape((width, rows), LOW),
            in_specs=[smem(), vmem()],
            out_specs=vmem(),
            scratch_shapes=[pltpu.VMEM((width, rows), LOW)],
            compiler_params=params(mib),
            cost_estimate=cost(rows / 256),
            name="spread",
        )(own, values)
    turned = pl.pallas_call(
        turn_body,
        out_shape=shape((width, rows), LOW),
        in_specs=[vmem()],
        out_specs=vmem(),
        compiler_params=params(mib),
        name="turn",
    )(values)
    blocks = turned.reshape(len(order), size, rows)
    return blocks[own[0] ^ jnp.array(order, jnp.int32)].reshape(width, rows)


def swap(values, axis, count, bit):
    return lax.ppermute(values, axis, [(i, i ^ (1 << bit)) for i in range(count)])


def halving(first, second, bits, count):
    kept = second + swap(first, "dp", count, bits[0])
    for bit in bits[1:]:
        middle = kept.shape[0] // 2
        kept = kept[middle:] + swap(kept[:middle], "dp", count, bit)
    return kept


def weight_sum(spread_left, right, bits, count):
    middle = spread_left.shape[0] // 2
    return halving(nn(spread_left[:middle], right), nn(spread_left[middle:], right), bits, count)


def per_device(
    count,
    inputs,
    datastore,
    lengths,
    indices,
    w_query,
    b_query,
    w_key,
    w_value,
    b_value,
    w_out,
    b_out,
    g_one,
    c_one,
    wc_query,
    bc_query,
    wc_key,
    wc_value,
    bc_value,
    wc_out,
    bc_out,
    g_two,
    c_two,
    w_up,
    b_up,
    w_down,
    b_down,
    g_three,
    c_three,
    cotangent,
):
    x = inputs[0]
    memory = datastore[0]
    q_scale = 1.0 / math.sqrt(HD)
    axes = count.bit_length() - 1
    order_a = list(range(axes))
    order_b = [1, 0] + list(range(2, axes))
    order_c = [2, 0, 1] + list(range(3, axes))
    own = lax.axis_index("dp").astype(jnp.int32).reshape(1)
    side = lax.axis_index("tensor")

    def line(vector):
        return vector.astype(F32).reshape(1, -1)

    def other_core(values):
        return lax.ppermute(values, "tensor", [(0, 1), (1, 0)])

    b_query, b_value, b_out, g_one, c_one, bc_query, bc_value, bc_out, g_two, c_two, b_up, b_down, g_three, c_three = map(
        line, (b_query, b_value, b_out, g_one, c_one, bc_query, bc_value, bc_out, g_two, c_two, b_up, b_down, g_three, c_three)
    )

    q, k, v, probs, inverse, ot, attended, self_part = self_forward(
        lengths, x, w_query, b_query, w_key, w_value, b_value, w_out
    )
    self_other = other_core(self_part)
    words = mask_words(indices[0])
    keys, values, keys_t, values_t = store_products(memory, wc_key, wc_value)
    unit_one, inv_one, one_low, cross_query, cross_probs, cross_sums, cross_ot, context, cross_part = cross_forward(
        x, self_part, self_other, b_out, g_one, c_one, wc_query, bc_query, words, keys, values_t, bc_value, wc_out
    )
    cross_other = other_core(cross_part)
    unit_two, inv_two, two_low, hidden, slope, ffn_part = ffn_forward(
        unit_one, g_one, c_one, cross_part, cross_other, bc_out, g_two, c_two, w_up, b_up, w_down
    )
    ffn_other = other_core(ffn_part)
    output, grad_three, grad_ffn, sums_three = norm_three(
        unit_two, g_two, c_two, ffn_part, ffn_other, b_down, g_three, c_three, cotangent[0]
    )

    grad_w_down = weight_sum(spread(own, grad_ffn, order_a), hidden, order_a, count)
    grad_pre = (nt(grad_ffn, w_down) * slope).astype(LOW)
    term_b_up = jnp.sum(grad_pre.astype(F32), axis=0)
    two_part = nt(grad_pre, w_up)
    two_other = other_core(two_part)
    grad_w_up = weight_sum(spread(own, two_low, order_b), grad_pre, order_b, count)

    grad_two, grad_cross, sums_two, sums_cross, grad_keys, grad_values, grad_cquery, one_part = cross_backward(
        grad_three, two_part, two_other, unit_two, inv_two, g_two, wc_out, cross_ot, cross_sums, cross_probs,
        values, keys_t, cross_query, wc_query,
    )
    one_other = other_core(one_part)
    grad_wc_out = weight_sum(spread(own, grad_cross, order_c), context, order_c, count)
    store_left = spread(own, memory, order_c)
    grad_wc_store = weight_sum(store_left, jnp.concatenate([grad_keys, grad_values], axis=1), order_c, count)
    grad_wc_query = weight_sum(spread(own, one_low, order_c), grad_cquery, order_c, count) * q_scale

    def store_term(which):
        rows = memory.shape[0] // 2
        left = lax.dynamic_slice_in_dim(grad_keys, which * rows, rows)
        right = lax.dynamic_slice_in_dim(grad_values, which * rows, rows)
        return nt(left, wc_key) + nt(right, wc_value)

    datastore_grad = (store_term(side) + other_core(store_term(1 - side)))[None]

    grad_one, grad_self, sums_one, sums_self, grad_q, grad_k, grad_v, in_part = self_backward(
        grad_two, one_part, one_other, unit_one, inv_one, g_one, w_out, ot, inverse, probs, q, k, v, w_query, w_key, w_value
    )
    input_grad = (grad_one + (in_part + other_core(in_part)))[None]
    grad_w_out = weight_sum(spread(own, grad_self, order_a), attended, order_a, count)
    grad_qkv = weight_sum(
        spread(own, x, order_b), jnp.concatenate([grad_q, grad_k, grad_v], axis=1), order_b, count
    )
    cols = w_query.shape[1]
    grad_w_query = grad_qkv[:, :cols] * q_scale
    grad_w_key = grad_qkv[:, cols : 2 * cols]
    grad_w_value = grad_qkv[:, 2 * cols :]

    pieces = [
        sums_self[0], sums_self[1], sums_one[2], sums_one[0], sums_one[1],
        sums_cross[1], sums_cross[0], sums_two[2], sums_two[0], sums_two[1],
        term_b_up, sums_three[2], sums_three[0], sums_three[1],
    ]
    widths = [piece.shape[0] // count for piece in pieces]
    table = jnp.concatenate([piece.reshape(count, -1) for piece in pieces], axis=1)
    table = table[own[0] ^ jnp.array(block_order(order_a), jnp.int32)]
    middle = count // 2
    table = halving(table[:middle], table[middle:], order_a, count)[0]
    starts = [sum(widths[:i]) for i in range(len(widths))]
    (
        grad_b_query, grad_b_value, grad_b_out, grad_g_one, grad_c_one,
        grad_bc_query, grad_bc_value, grad_bc_out, grad_g_two, grad_c_two,
        grad_b_up, grad_b_down, grad_g_three, grad_c_three,
    ) = [table[start : start + size] for start, size in zip(starts, widths)]
    return (
        output[None],
        input_grad,
        datastore_grad,
        grad_w_query,
        grad_b_query,
        grad_w_key,
        grad_w_value,
        grad_b_value,
        grad_w_out.T,
        grad_b_out,
        grad_g_one,
        grad_c_one,
        grad_wc_query,
        grad_bc_query,
        grad_wc_store[:, :cols],
        grad_wc_store[:, cols:],
        grad_bc_value,
        grad_wc_out.T,
        grad_bc_out,
        grad_g_two,
        grad_c_two,
        grad_w_up,
        grad_b_up,
        grad_w_down.T,
        grad_b_down,
        grad_g_three,
        grad_c_three,
    )


def solution(mesh):
    return jax.shard_map(
        functools.partial(per_device, mesh.shape["dp"]),
        mesh=mesh,
        in_specs=(
            P("dp", None, None),
            P("dp", None, None),
            P("dp"),
            P("dp", None, None),
            P(None, "tensor"),
            P("tensor"),
            P(None, "tensor"),
            P(None, "tensor"),
            P("tensor"),
            P("tensor", None),
            P(),
            P(),
            P(),
            P(None, "tensor"),
            P("tensor"),
            P(None, "tensor"),
            P(None, "tensor"),
            P("tensor"),
            P("tensor", None),
            P(),
            P(),
            P(),
            P(None, "tensor"),
            P("tensor"),
            P("tensor", None),
            P(),
            P(),
            P(),
            P("dp", None, None),
        ),
        out_specs=(
            P("dp", None, None),
            P("dp", None, None),
            P("dp", "tensor", None),
            P("dp", "tensor"),
            P(("tensor", "dp")),
            P("dp", "tensor"),
            P("dp", "tensor"),
            P(("tensor", "dp")),
            P("tensor", "dp"),
            P("dp"),
            P("dp"),
            P("dp"),
            P("dp", "tensor"),
            P(("tensor", "dp")),
            P("dp", "tensor"),
            P("dp", "tensor"),
            P(("tensor", "dp")),
            P("tensor", "dp"),
            P("dp"),
            P("dp"),
            P("dp"),
            P("dp", "tensor"),
            P(("tensor", "dp")),
            P("tensor", "dp"),
            P("dp"),
            P("dp"),
            P("dp"),
        ),
        check_vma=False,
    )
```

```python
import functools
import math

import jax
import jax.numpy as jnp
from jax import lax
from jax.experimental import pallas as pl
from jax.experimental.pallas import tpu as pltpu
from jax.sharding import PartitionSpec as P

HD = 64
NEG = -1e30
EPS = 1e-05
WORDS = 256
MIB = 1 << 20

F32 = jnp.float32
DP = "dp"
TENSOR = "tensor"
LOW = jnp.bfloat16


def nn(left, right):
    return lax.dot_general(left, right, (((1,), (0,)), ((), ())), preferred_element_type=F32)


def nt(left, right):
    return lax.dot_general(left, right, (((1,), (1,)), ((), ())), preferred_element_type=F32)


def tn(left, right):
    return lax.dot_general(left, right, (((0,), (0,)), ((), ())), preferred_element_type=F32)


def flip(values):
    return values.astype(F32).T


def row(ref):
    return ref[...].astype(F32).reshape(1, -1)


def spread_row(ref, out):
    values = row(ref)
    wide = out.shape[1]
    for i in range(out.shape[0]):
        out[i : i + 1, :] = values[:, i * wide : (i + 1) * wide]


def shape(dims, kind=F32):
    return jax.ShapeDtypeStruct(dims, kind)


VMEM = pl.BlockSpec(memory_space=pltpu.VMEM)
SMEM = pl.BlockSpec(memory_space=pltpu.SMEM)
ANY = pl.BlockSpec(memory_space=pl.ANY)


def whole(dims):
    return pl.BlockSpec(dims, lambda i: (0,) * len(dims), pipeline_mode=pl.Buffered(1))


def kept(dims):
    return pl.BlockSpec(dims, lambda i: (0,) * len(dims))


WEIGHTS = {"cross_b": 10000000000, "fold_c": 1, "fold_b": 6000000000, "self_b": 3000000000, "fold_d": 20000000000, "ffn_b": 6000000000, "outer": 10000000000, "fold": 40000000000, "": 1}


def weight_of(name):
    return next(weight for prefix, weight in WEIGHTS.items() if name.startswith(prefix))


class Chain:
    def __init__(self):
        self.token = None

    def __call__(self, body, args, ins, shapes, outs, mib, name, grid=None, scratch=()):
        given = len(args)
        extra = [] if self.token is None else [pltpu.with_memory_space_constraint(self.token, pltpu.HBM)]

        def kernel(*refs):
            refs = list(refs)
            token = refs.pop(given + len(extra) + len(shapes))
            del refs[given : given + len(extra)]
            body(*refs)
            token[...] = jnp.zeros_like(token)

        more = {} if grid is None else {"grid": (grid,)}
        args = [
            pltpu.with_memory_space_constraint(arg, pltpu.HBM) if spec.memory_space in (None, pl.ANY) else arg
            for arg, spec in zip(args, ins)
        ]
        shapes = [
            pltpu.HBM(out.shape, out.dtype) if spec.memory_space is None else out for out, spec in zip(shapes, outs)
        ]
        results = pl.pallas_call(
            kernel,
            out_shape=(*shapes, pltpu.HBM((8, 128), F32)),
            in_specs=[*ins, *([ANY] * len(extra))],
            out_specs=(*outs, whole((8, 128)) if grid else pl.BlockSpec((8, 128))),
            scratch_shapes=list(scratch),
            compiler_params=pltpu.CompilerParams(vmem_limit_bytes=mib * MIB),
            cost_estimate=pl.CostEstimate(flops=weight_of(name), bytes_accessed=1, transcendentals=0),
            name=name,
            **more,
        )(*args, *extra)
        self.token = results[-1]
        return results[:-1]


def norm_parts(values):
    average = jnp.mean(values, axis=-1, keepdims=True)
    centred = values - average
    variance = jnp.mean(centred * centred, axis=-1, keepdims=True)
    inverse = lax.rsqrt(variance + EPS)
    return centred * inverse, inverse


def norm_back(grad, gain, unit, inverse):
    scaled = grad * gain
    first = jnp.mean(scaled, axis=-1, keepdims=True)
    second = jnp.mean(scaled * unit, axis=-1, keepdims=True)
    return inverse * (scaled - first - unit * second)


def rows_of_half(values, half):
    place = lax.broadcasted_iota(jnp.int32, values.shape, 0)
    return jnp.where((place // HD) == half, values, jnp.zeros_like(values))


def lanes_of_half(values, half):
    place = lax.broadcasted_iota(jnp.int32, values.shape, 1)
    return jnp.where((place // HD) == half, values, jnp.zeros_like(values))


def self_forward_body(
    length, x, wq, bq, wk, wv, bv, wo,
    q_out, k_out, v_out, p_out, inv_out, ot_out, att_out, part_out,
    bias, q_low, k_low, v_low, probs, done,
):
    rows = x.shape[0]
    heads = wq.shape[1] // HD
    q_scale = 1.0 / math.sqrt(HD)
    copies = []

    def leave(source, target):
        copy = pltpu.make_async_copy(source, target, done.at[len(copies)])
        copy.start()
        copies.append(copy)

    x_low = x[...]
    q = ((nn(x_low, wq[...]) + row(bq)) * q_scale).astype(LOW)
    k = nn(x_low, wk[...]).astype(LOW)
    v = (nn(x_low, wv[...]) + row(bv)).astype(LOW)
    q_low[...] = q
    k_low[...] = k
    v_low[...] = v
    leave(q_low, q_out)
    leave(k_low, k_out)
    leave(v_low, v_out)
    qt = flip(q).astype(LOW)
    vt = flip(v).astype(LOW)
    key = lax.broadcasted_iota(jnp.int32, (rows, rows), 0)
    query = lax.broadcasted_iota(jnp.int32, (rows, rows), 1)
    bias[...] = jnp.where((key <= query) & (key < length[0]), 0.0, NEG)
    for head in range(heads):
        pair, half = head // 2, head % 2
        lanes = slice(pair * 2 * HD, (pair + 1) * 2 * HD)
        own = slice(head * HD, (head + 1) * HD)
        scores = nn(k[:, lanes], rows_of_half(qt[lanes], half)) + bias[...]
        top = jnp.max(scores, axis=0, keepdims=True)
        grown = jnp.exp(scores - top)
        inverse = 1.0 / jnp.sum(grown, axis=0, keepdims=True)
        low = grown.astype(LOW)
        probs[head] = low
        leave(probs.at[head], p_out.at[head])
        inv_out[pair, half : half + 1, :] = inverse
        ot_out[own, :] = nn(vt[own], low) * inverse
    attended = ot_out[...].T.astype(LOW)
    att_out[...] = attended
    part_out[...] = nn(attended, wo[...])
    for copy in copies:
        copy.wait()


def self_forward(chain, length, x, wq, bq, wk, wv, bv, wo):
    rows, width = x.shape
    cols = wq.shape[1]
    heads = cols // HD
    pairs = heads // 2
    side = whole((width, cols))
    return chain(
        self_forward_body,
        (length, x, wq, bq, wk, wv, bv, wo),
        [SMEM, whole((rows, width)), side, whole((cols,)), side, side, whole((cols,)), whole((cols, width))],
        (
            pltpu.HBM((rows, cols), LOW),
            pltpu.HBM((rows, cols), LOW),
            pltpu.HBM((rows, cols), LOW),
            pltpu.HBM((heads, rows, rows), LOW),
            shape((pairs, 2, rows)),
            shape((cols, rows)),
            shape((rows, cols), LOW),
            shape((rows, width)),
        ),
        (
            ANY, ANY, ANY, ANY,
            whole((pairs, 2, rows)),
            whole((cols, rows)),
            whole((rows, cols)),
            VMEM,
        ),
        28,
        "self_forward",
        grid=1,
        scratch=[
            pltpu.VMEM((rows, rows), F32),
            pltpu.VMEM((rows, cols), LOW),
            pltpu.VMEM((rows, cols), LOW),
            pltpu.VMEM((rows, cols), LOW),
            pltpu.VMEM((heads, rows, rows), LOW),
            pltpu.SemaphoreType.DMA((heads + 3,)),
        ],
    )


def mask_body(picks, words, sums):
    step = pl.program_id(0)
    block = picks.shape[0]
    up = lax.broadcasted_iota(jnp.int32, (256, 256), 0)
    across = lax.broadcasted_iota(jnp.int32, (256, 256), 1)
    same = (up & 15) == (across & 15)
    for part in range(block // 16):
        index = picks[part * 16 : (part + 1) * 16, :]
        bit = lax.shift_left(jnp.ones_like(index), index >> 8).astype(F32).astype(LOW)
        upper = ((index >> 4) & 15).astype(F32).astype(LOW)
        lower = (index & 15).astype(F32).astype(LOW)
        zero = jnp.zeros_like(bit)
        one = jnp.ones_like(bit)
        left = jnp.concatenate([jnp.where(upper == c, bit, zero) for c in range(16)], axis=0)
        right = jnp.concatenate([jnp.where(lower == c, one, zero) for c in range(16)], axis=0)
        cross = jnp.where(same, nt(left, right), 0.0).astype(LOW)
        start = pl.multiple_of(step * block + part * 16, 16)
        for c in range(16):
            sums[pl.ds(start, 16), c * 256 : (c + 1) * 256] = cross[c * 16 : (c + 1) * 16, :]

    @pl.when(step == pl.num_programs(0) - 1)
    def _():
        word = lax.broadcasted_iota(jnp.int32, (256, 4096), 0)
        place = lax.broadcasted_iota(jnp.int32, (256, 4096), 1)
        fold = jnp.where((place >> 4) == word, 1.0, 0.0).astype(LOW)
        words[...] = nt(fold, sums[...]).astype(jnp.int32)


def mask_words(chain, picks):
    rows, chosen = picks.shape
    block = math.gcd(rows, 128)
    return chain(
        mask_body,
        (picks,),
        [pl.BlockSpec((block, chosen), lambda i: (i, 0))],
        (shape((WORDS, rows), jnp.int32),),
        (whole((WORDS, rows)),),
        16,
        "mask_words",
        grid=rows // block,
        scratch=[pltpu.VMEM((rows, 16 * 256), LOW)],
    )[0]


def put_pairs(out, values):
    high = values.astype(LOW)
    rest = (values - high.astype(F32)).astype(LOW)
    pair = 2 * HD
    for i in range(values.shape[1] // pair):
        out[:, 2 * i * pair : (2 * i + 1) * pair] = high[:, i * pair : (i + 1) * pair]
        out[:, (2 * i + 1) * pair : (2 * i + 2) * pair] = rest[:, i * pair : (i + 1) * pair]


def put_heads(out, values):
    high = values.astype(LOW)
    rest = (values - high.astype(F32)).astype(LOW)
    for i in range(values.shape[0] // HD):
        out[2 * i * HD : (2 * i + 1) * HD, :] = high[i * HD : (i + 1) * HD, :]
        out[(2 * i + 1) * HD : (2 * i + 2) * HD, :] = rest[i * HD : (i + 1) * HD, :]


def store_body(memory, wk, wv, k_out, vt_out):
    low = memory[...]
    put_pairs(k_out, nn(low, wk[...]))
    turned = (((0,), (1,)), ((), ()))
    put_heads(vt_out, lax.dot_general(wv[...], low, turned, preferred_element_type=F32))


def store_turned_body(memory, wk, wv, v_out, kt_out):
    low = memory[...]
    put_pairs(v_out, nn(low, wv[...]))
    turned = (((0,), (1,)), ((), ()))
    put_heads(kt_out, lax.dot_general(wk[...], low, turned, preferred_element_type=F32))


def store_products(chain, memory, wk, wv, first):
    entries, width = memory.shape
    cols = wk.shape[1]
    block = 512
    return chain(
        store_body if first else store_turned_body,
        (memory, wk, wv),
        [pl.BlockSpec((block, width), lambda i: (i, 0)), whole((width, cols)), whole((width, cols))],
        (shape((entries, 2 * cols), LOW), shape((2 * cols, entries), LOW)),
        (pl.BlockSpec((block, 2 * cols), lambda i: (i, 0)), pl.BlockSpec((2 * cols, block), lambda i: (0, i))),
        16,
        "store_products" if first else "store_turned",
        grid=entries // block,
    )


def cross_forward_body(
    x, own, other, b_out, g_one, c_one, wq, bq, words, keys, values_t, bv, wo,
    unit_out, inv_out, turn_out, q_out, p_out, sum_out, ot_out, ctx_out, part_out,
    qt, bias, scores, keys_held, values_held, probs, loads, leaves,
):
    q_scale = 1.0 / math.sqrt(HD)
    entries = keys.shape[0]
    heads = wq.shape[1] // HD
    chunk = 512
    wide = 4 * HD

    def load(pair):
        lanes = pl.ds(pl.multiple_of(pair * wide, wide), wide)
        return (
            pltpu.make_async_copy(keys.at[:, lanes], keys_held.at[pair], loads.at[0, pair]),
            pltpu.make_async_copy(values_t.at[lanes, :], values_held.at[pair], loads.at[1, pair]),
        )

    def leave(pair, half):
        return pltpu.make_async_copy(probs.at[half], p_out.at[2 * pair + half], leaves.at[half])

    for pair in range(heads // 2):
        for copy in load(pair):
            copy.start()
    total = x[...].astype(F32) + (own[...] + other[...] + row(b_out))
    unit, inverse = norm_parts(total)
    unit_out[...] = unit
    inv_out[...] = inverse
    low = (unit * row(g_one) + row(c_one)).astype(LOW)
    turn_out[...] = flip(low).astype(LOW)
    q = ((nn(low, wq[...]) + row(bq)) * q_scale).astype(LOW)
    q_out[...] = q
    qt[...] = flip(q).astype(LOW)
    held = words[...]
    for part in range(entries // WORDS):
        bias[part * WORDS : (part + 1) * WORDS, :] = jnp.where(((held >> part) & 1) == 1, 0.0, NEG)

    def one_pair(pair, carry):
        for copy in load(pair):
            copy.wait()
        pair_rows = qt[pl.ds(pl.multiple_of(pair * 2 * HD, 2 * HD), 2 * HD), :]
        for half in range(2):
            query = rows_of_half(pair_rows, half)
            query = jnp.concatenate([query, query], axis=0)
            top = None
            for part in range(entries // chunk):
                span = slice(part * chunk, (part + 1) * chunk)
                piece = nn(keys_held[pair, span, :], query) + bias[span, :]
                scores[half, span, :] = piece
                peak = jnp.max(piece.reshape(chunk // 8, 8, -1), axis=0)
                top = peak if top is None else jnp.maximum(top, peak)
            top = jnp.max(top, axis=0, keepdims=True)

            @pl.when(pair > 0)
            def _():
                leave(pair - 1, half).wait()

            total = pooled = None
            for part in range(entries // chunk):
                span = slice(part * chunk, (part + 1) * chunk)
                grown = jnp.exp(scores[half, span, :] - top)
                low = grown.astype(LOW)
                probs[half, span, :] = low
                mass = jnp.sum(grown.reshape(chunk // 8, 8, -1), axis=0)
                term = nn(values_held[pair, half * 2 * HD : (half + 1) * 2 * HD, span], low)
                total, pooled = (mass, term) if total is None else (total + mass, pooled + term)
            leave(pair, half).start()
            inverse = 1.0 / jnp.sum(total, axis=0, keepdims=True)
            head = 2 * pair + half
            sum_out[pl.ds(head, 1), :] = inverse
            ot_out[pl.ds(pl.multiple_of(head * HD, HD), HD), :] = (pooled[:HD] + pooled[HD:]) * inverse
        return carry

    lax.fori_loop(0, heads // 2, one_pair, 0)
    context = (ot_out[...].T + row(bv)).astype(LOW)
    ctx_out[...] = context
    part_out[...] = nn(context, wo[...])
    for half in range(2):
        leave(heads // 2 - 1, half).wait()


def cross_forward(chain, x, own, other, b_out, g_one, c_one, wq, bq, words, keys, values_t, bv, wo):
    rows, width = x.shape
    entries = keys.shape[0]
    cols = wq.shape[1]
    heads = cols // HD
    line = whole((width,))
    thin = whole((cols,))
    return chain(
        cross_forward_body,
        (x, own, other, b_out, g_one, c_one, wq, bq, words, keys, values_t, bv, wo),
        [whole((rows, width)), VMEM, VMEM, line, line, line, whole((width, cols)), thin, whole((WORDS, rows)),
         ANY, ANY, thin, whole((cols, width))],
        (
            shape((rows, width)),
            shape((rows, 1)),
            shape((width, rows), LOW),
            shape((rows, cols), LOW),
            pltpu.HBM((heads, entries, rows), LOW),
            shape((heads, rows)),
            shape((cols, rows)),
            shape((rows, cols), LOW),
            shape((rows, width)),
        ),
        (VMEM, whole((rows, 1)), VMEM, VMEM, ANY, VMEM, whole((cols, rows)), VMEM, VMEM),
        38,
        "cross_forward",
        grid=1,
        scratch=[
            pltpu.VMEM((cols, rows), LOW),
            pltpu.VMEM((entries, rows), F32),
            pltpu.VMEM((2, entries, rows), F32),
            pltpu.VMEM((heads // 2, entries, 4 * HD), LOW),
            pltpu.VMEM((heads // 2, 4 * HD, entries), LOW),
            pltpu.VMEM((2, entries, rows), LOW),
            pltpu.SemaphoreType.DMA((2, heads // 2)),
            pltpu.SemaphoreType.DMA((2,)),
        ],
    )


def ffn_forward_body(
    unit_one, g_one, c_one, own, other, b_out, g_two, c_two, w_up, b_up, w_down,
    unit_out, inv_out, turn_out, hid_out, slope_out, part_out, low_two, bias,
):
    step = pl.program_id(0)

    @pl.when(step == 0)
    def _():
        total = unit_one[...] * row(g_one) + row(c_one) + (own[...] + other[...] + row(b_out))
        unit, inverse = norm_parts(total)
        unit_out[...] = unit
        inv_out[...] = inverse
        low = (unit * row(g_two) + row(c_two)).astype(LOW)
        low_two[...] = low
        spread_row(b_up, bias)
        turn_out[...] = flip(low).astype(LOW)

    pre = nn(low_two[...], w_up[...]) + bias[pl.ds(step, 1), :]
    below = 0.5 * (1.0 + lax.erf(pre * math.sqrt(0.5)))
    density = jnp.exp(-0.5 * pre * pre) * (1.0 / math.sqrt(2.0 * math.pi))
    lanes = pl.ds(pl.multiple_of(step * pre.shape[1], pre.shape[1]), pre.shape[1])
    slope_out[...] = below + pre * density
    hidden = (pre * below).astype(LOW)
    hid_out[:, lanes] = hidden
    term = nn(hidden, w_down[...])

    @pl.when(step == 0)
    def _():
        part_out[...] = term

    @pl.when(step > 0)
    def _():
        part_out[...] += term


def ffn_forward(chain, unit_one, g_one, c_one, own, other, b_out, g_two, c_two, w_up, b_up, w_down):
    rows, width = unit_one.shape
    units = w_up.shape[1]
    block = 512
    return chain(
        ffn_forward_body,
        (unit_one, g_one, c_one, own, other, b_out, g_two, c_two, w_up, b_up, w_down),
        [
            VMEM,
            whole((width,)),
            whole((width,)),
            VMEM,
            VMEM,
            whole((width,)),
            whole((width,)),
            whole((width,)),
            pl.BlockSpec((width, block), lambda i: (0, i)),
            whole((units,)),
            pl.BlockSpec((block, width), lambda i: (i, 0)),
        ],
        (
            shape((rows, width)),
            shape((rows, 1)),
            shape((width, rows), LOW),
            shape((rows, units), LOW),
            shape((rows, units)),
            shape((rows, width)),
        ),
        (VMEM, whole((rows, 1)), whole((width, rows)), VMEM, pl.BlockSpec((rows, block), lambda i: (0, i)), VMEM),
        20,
        "ffn_forward",
        grid=units // block,
        scratch=[pltpu.VMEM((rows, width), LOW), pltpu.VMEM((units // block, block), F32)],
    )


def norm_three_body(unit_two, g_two, c_two, own, other, b_down, g_three, c_three, cotangent, out, grad, low, turn, sums):
    step = pl.program_id(0)
    block = out.shape[0]
    span = pl.ds(pl.multiple_of(step * block, block), block)
    total = unit_two[span, :] * row(g_two) + row(c_two) + (own[span, :] + other[span, :] + row(b_down))
    unit, inverse = norm_parts(total)
    out[...] = (unit * row(g_three) + row(c_three)).astype(LOW)
    seed = cotangent[...].astype(F32)
    back = norm_back(seed, row(g_three), unit, inverse)
    rounded = back.astype(LOW)
    grad[span, :] = back
    low[span, :] = rounded
    turn[:, span] = flip(rounded).astype(LOW)

    @pl.when(step == 0)
    def _():
        sums[...] = jnp.zeros_like(sums)

    sums[0:1, :] += jnp.sum(seed * unit, axis=0, keepdims=True)
    sums[1:2, :] += jnp.sum(seed, axis=0, keepdims=True)
    sums[2:3, :] += jnp.sum(rounded.astype(F32), axis=0, keepdims=True)


def norm_three(chain, *args):
    rows, width = args[0].shape
    block = rows // 2
    tall = pl.BlockSpec((block, width), lambda i: (i, 0))
    line = whole((width,))
    return chain(
        norm_three_body,
        args,
        [VMEM, line, line, VMEM, VMEM, line, line, line, tall],
        (
            shape((rows, width), LOW),
            shape((rows, width)),
            shape((rows, width), LOW),
            shape((width, rows), LOW),
            shape((3, width)),
        ),
        (tall, VMEM, VMEM, VMEM, VMEM),
        12,
        "norm_three",
        grid=2,
    )


def ffn_backward_body(grad, w_down, slope, w_up, pre_out, sum_out, part_out):
    step = pl.program_id(0)
    block = w_down.shape[0]
    lanes = pl.ds(pl.multiple_of(step * block, block), block)
    back = (nt(grad[...], w_down[...]) * slope[...]).astype(LOW)
    pre_out[:, lanes] = back
    sum_out[:, lanes] = jnp.sum(back.astype(F32), axis=0, keepdims=True)
    term = nt(back, w_up[...])

    @pl.when(step == 0)
    def _():
        part_out[...] = term

    @pl.when(step > 0)
    def _():
        part_out[...] += term


def ffn_backward(chain, grad, w_down, slope, w_up):
    rows, width = grad.shape
    units = w_up.shape[1]
    block = 512
    return chain(
        ffn_backward_body,
        (grad, w_down, slope, w_up),
        [
            VMEM,
            pl.BlockSpec((block, width), lambda i: (i, 0)),
            pl.BlockSpec((rows, block), lambda i: (0, i)),
            pl.BlockSpec((width, block), lambda i: (0, i)),
        ],
        (shape((rows, units), LOW), shape((1, units)), shape((rows, width))),
        (VMEM, whole((1, units)), VMEM),
        12,
        "ffn_backward",
        grid=units // block,
    )


def cross_backward_body(
    grad_three, own, other, unit_two, inv_two, g_two, wo, ot, sums, probs, values, keys_t, query, wq,
    grad_out, turn_out, norm_sums, head_sums, dk_out, dv_out, dq_out, part_out,
    dctx_t, dq_t, change, grad_held, probs_held, values_held, keys_held, loads, brings, done,
):
    q_scale = 1.0 / math.sqrt(HD)
    entries = values.shape[0]
    cols = wq.shape[1]
    heads = cols // HD
    chunk = 512
    wide = 4 * HD

    def load(pair):
        lanes = pl.ds(pl.multiple_of(pair * wide, wide), wide)
        return (
            pltpu.make_async_copy(values.at[:, lanes], values_held.at[pair], loads.at[0, pair]),
            pltpu.make_async_copy(keys_t.at[lanes, :], keys_held.at[pair], loads.at[1, pair]),
        )

    def bring(pair, half):
        return pltpu.make_async_copy(probs.at[2 * pair + half], probs_held.at[half], brings.at[half])

    bring(0, 0).start()
    for pair in range(heads // 2):
        for copy in load(pair):
            copy.start()
        if pair == 0:
            bring(0, 1).start()
    grad_in = grad_three[...] + (own[...] + other[...])
    unit = unit_two[...]
    grad = norm_back(grad_in, row(g_two), unit, inv_two[...])
    grad_held[...] = grad
    keep = pltpu.make_async_copy(grad_held, grad_out, done)
    keep.start()
    low = grad.astype(LOW)
    turn_out[...] = flip(low).astype(LOW)
    norm_sums[0:1, :] = jnp.sum(grad_in * unit, axis=0, keepdims=True)
    norm_sums[1:2, :] = jnp.sum(grad_in, axis=0, keepdims=True)
    norm_sums[2:3, :] = jnp.sum(low.astype(F32), axis=0, keepdims=True)
    dctx_t[...] = nt(wo[...], low)
    head_sums[0:1, :cols] = jnp.sum(dctx_t[...].T, axis=0, keepdims=True)

    def one_pair(pair, carry):
        for copy in load(pair):
            copy.wait()
        lanes = pl.ds(pl.multiple_of(pair * 2 * HD, 2 * HD), 2 * HD)
        pair_query = query[:, lanes]
        for half in range(2):
            head = 2 * pair + half
            own_rows = pl.ds(pl.multiple_of(head * HD, HD), HD)
            scaled = (dctx_t[own_rows, :] * sums[pl.ds(head, 1), :]).astype(LOW)
            inner = jnp.sum(scaled.astype(F32) * ot[own_rows, :], axis=0, keepdims=True)
            empty = jnp.zeros_like(scaled)
            grad_rows = jnp.concatenate([scaled, empty] if half == 0 else [empty, scaled], axis=0)
            own_grad = flip(grad_rows).astype(LOW)
            grad_rows = jnp.concatenate([grad_rows, grad_rows], axis=0)
            own_query = lanes_of_half(pair_query, half)
            bring(pair, half).wait()
            for part in range(entries // chunk):
                span = slice(part * chunk, (part + 1) * chunk)
                low_probs = probs_held[half, span, :]
                shift = nn(values_held[pair, span, :], grad_rows) - inner
                delta = (low_probs.astype(F32) * shift).astype(LOW)
                change[half, span, :] = delta
                k_term = nn(delta, own_query).astype(LOW)
                v_term = nn(low_probs, own_grad).astype(LOW)
                if half == 0:
                    dk_out[span, lanes] = k_term
                    dv_out[span, lanes] = v_term
                else:
                    dk_out[span, lanes] = dk_out[span, lanes] + k_term
                    dv_out[span, lanes] = dv_out[span, lanes] + v_term

            @pl.when(pair + 1 < heads // 2)
            def _():
                bring(pair + 1, half).start()

            both = nn(keys_held[pair, half * 2 * HD : (half + 1) * 2 * HD, :], change[half])
            dq_t[own_rows, :] = both[:HD] + both[HD:]
        return carry

    lax.fori_loop(0, heads // 2, one_pair, 0)
    dq = dq_t[...].T.astype(LOW)
    dq_out[...] = dq
    head_sums[0:1, cols:] = jnp.sum(dq.astype(F32), axis=0, keepdims=True) * q_scale
    part_out[...] = nt(dq, wq[...]) * q_scale
    keep.wait()


def cross_backward(chain, *args):
    rows, width = args[0].shape
    entries = args[10].shape[0]
    cols = args[13].shape[1]
    heads = cols // HD
    return chain(
        cross_backward_body,
        args,
        [VMEM, VMEM, VMEM, VMEM, whole((rows, 1)), whole((width,)), whole((cols, width)), whole((cols, rows)), VMEM,
         ANY, ANY, ANY, VMEM, whole((width, cols))],
        (
            pltpu.HBM((rows, width), F32),
            shape((width, rows), LOW),
            shape((3, width)),
            shape((1, 2 * cols)),
            shape((entries, cols), LOW),
            shape((entries, cols), LOW),
            shape((rows, cols), LOW),
            shape((rows, width)),
        ),
        (ANY, VMEM, whole((3, width)), whole((1, 2 * cols)), VMEM, VMEM, VMEM, VMEM),
        32,
        "cross_backward",
        grid=1,
        scratch=[
            pltpu.VMEM((cols, rows), F32),
            pltpu.VMEM((cols, rows), F32),
            pltpu.VMEM((2, entries, rows), LOW),
            pltpu.VMEM((rows, width), F32),
            pltpu.VMEM((2, entries, rows), LOW),
            pltpu.VMEM((heads // 2, entries, 4 * HD), LOW),
            pltpu.VMEM((heads // 2, 4 * HD, entries), LOW),
            pltpu.SemaphoreType.DMA((2, heads // 2)),
            pltpu.SemaphoreType.DMA((2,)),
            pltpu.SemaphoreType.DMA,
        ],
    )


def self_backward_body(
    grad_two, own, other, unit_one, inv_one, g_one, wo, ot, inverse, probs, q, k, v, wq, wk, wv,
    grad_out, turn_out, norm_sums, head_sums, dq_out, dk_out, dv_out, part_out,
    datt_t, grad_held, done,
):
    step = pl.program_id(0)
    q_scale = 1.0 / math.sqrt(HD)
    cols = datt_t.shape[0]

    @pl.when(step == 0)
    def _():
        grad_in = grad_two[...] + (own[...] + other[...])
        unit = unit_one[...]
        grad = norm_back(grad_in, row(g_one), unit, inv_one[...])
        grad_held[...] = grad
        pltpu.make_async_copy(grad_held, grad_out, done).start()
        low = grad.astype(LOW)
        turn_out[...] = flip(low).astype(LOW)
        norm_sums[0:1, :] = jnp.sum(grad_in * unit, axis=0, keepdims=True)
        norm_sums[1:2, :] = jnp.sum(grad_in, axis=0, keepdims=True)
        norm_sums[2:3, :] = jnp.sum(low.astype(F32), axis=0, keepdims=True)
        datt_t[...] = nt(wo[...], low)

    pair_grad = datt_t[pl.ds(pl.multiple_of(step * 2 * HD, 2 * HD), 2 * HD), :]
    place = lax.broadcasted_iota(jnp.int32, pair_grad.shape, 0)
    scaled = pair_grad * jnp.where(place < HD, inverse[0, 0:1, :], inverse[0, 1:2, :])
    scaled_low = scaled.astype(LOW)
    weighed = scaled_low.astype(F32) * ot[...]
    scaled_rows = flip(scaled_low).astype(LOW)
    pair_query = q[...]
    pair_values = v[...]
    keys_t = flip(k[...]).astype(LOW)
    dk = None
    dv = None
    dq_t = []
    for half in range(2):
        inner = jnp.sum(weighed[half * HD : (half + 1) * HD, :], axis=0, keepdims=True)
        low_probs = probs[half]
        shift = nn(pair_values, rows_of_half(scaled_low, half)) - inner
        delta = (low_probs.astype(F32) * shift).astype(LOW)
        k_term = nn(delta, lanes_of_half(pair_query, half))
        v_term = nn(low_probs, lanes_of_half(scaled_rows, half))
        dk = k_term if dk is None else dk + k_term
        dv = v_term if dv is None else dv + v_term
        dq_t.append(nn(keys_t[half * HD : (half + 1) * HD], delta))
    dq = jnp.concatenate(dq_t, axis=0).T.astype(LOW)
    dk_low = dk.astype(LOW)
    dv_low = dv.astype(LOW)
    lanes = pl.ds(pl.multiple_of(step * 2 * HD, 2 * HD), 2 * HD)
    dq_out[:, lanes] = dq
    dk_out[:, lanes] = dk_low
    dv_out[:, lanes] = dv_low
    later = pl.ds(pl.multiple_of(cols + step * 2 * HD, 2 * HD), 2 * HD)
    head_sums[0:1, lanes] = jnp.sum(dq.astype(F32), axis=0, keepdims=True) * q_scale
    head_sums[0:1, later] = jnp.sum(dv_low.astype(F32), axis=0, keepdims=True)
    term = nt(dq, wq[...]) * q_scale + nt(
        jnp.concatenate([dk_low, dv_low], axis=1), jnp.concatenate([wk[...], wv[...]], axis=1)
    )

    @pl.when(step == 0)
    def _():
        part_out[...] = term

    @pl.when(step > 0)
    def _():
        part_out[...] += term

    @pl.when(step == pl.num_programs(0) - 1)
    def _():
        pltpu.make_async_copy(grad_held, grad_out, done).wait()


def self_backward(chain, *args):
    rows, width = args[0].shape
    cols = args[10].shape[1]
    pairs = cols // (2 * HD)
    tall = pl.BlockSpec((rows, 2 * HD), lambda i: (0, i))
    side = pl.BlockSpec((width, 2 * HD), lambda i: (0, i))
    return chain(
        self_backward_body,
        args,
        [
            whole((rows, width)),
            VMEM,
            VMEM,
            whole((rows, width)),
            whole((rows, 1)),
            whole((width,)),
            whole((cols, width)),
            pl.BlockSpec((2 * HD, rows), lambda i: (i, 0)),
            pl.BlockSpec((1, 2, rows), lambda i: (i, 0, 0)),
            pl.BlockSpec((2, rows, rows), lambda i: (i, 0, 0)),
            tall, tall, tall, side, side, side,
        ],
        (
            pltpu.HBM((rows, width), F32),
            shape((width, rows), LOW),
            shape((3, width)),
            shape((1, 2 * cols)),
            shape((rows, cols), LOW),
            shape((rows, cols), LOW),
            shape((rows, cols), LOW),
            shape((rows, width)),
        ),
        (ANY, VMEM, whole((3, width)), whole((1, 2 * cols)), VMEM, VMEM, VMEM, VMEM),
        18,
        "self_backward",
        grid=pairs,
        scratch=[pltpu.VMEM((cols, rows), F32), pltpu.VMEM((rows, width), F32), pltpu.SemaphoreType.DMA],
    )


def store_term_body(side, keys, values, wk, wv, out, *, flipped):
    rows = out.shape[0]
    which = 1 - side[0] if flipped else side[0]
    span = pl.ds(pl.multiple_of(which * rows, rows), rows)
    out[...] = nt(keys[span, :], wk[...]) + nt(values[span, :], wv[...])


def store_sum_body(side, keys, values, wk, wv, other, out):
    store_term_body(side, keys, values, wk, wv, out, flipped=False)
    out[...] += other[...]


def turn_body(values, out):
    out[...] = flip(values[...]).astype(LOW)


def turn(chain, values):
    rows, width = values.shape
    block = min(rows, 512)
    return chain(
        turn_body,
        (values,),
        [pl.BlockSpec((block, width), lambda i: (i, 0))],
        (shape((width, rows), LOW),),
        (pl.BlockSpec((width, block), lambda i: (0, i)),),
        16,
        "turn",
        grid=rows // block,
    )[0]


BITS = {"x": 0, "y": 1, "l": 2, "h": 3}

PIECES = {
    "a": ("lhxy", (("down", 0, 11),)),
    "b": ("xlyh", (("down", 11, 12), ("up", 0, 12))),
    "c": ("yxlh", (("key", 0, 3), ("value", 0, 3), ("mix", 0, 3), ("ask", 0, 3))),
    "d": ("yxlh", (("q", 0, 3), ("k", 0, 3))),
    "e": ("xlyh", (("v", 0, 3), ("out", 0, 3))),
}
EXTRA_PIECE = "d"
UNIT = 128


def bits_of(letters, count):
    total = count.bit_length() - 1
    chosen = [BITS[letter] for letter in letters if BITS[letter] < total]
    return chosen + [bit for bit in range(total) if bit not in chosen]


def block_order(bits):
    count = len(bits)
    return [
        sum((1 - ((place >> (count - 1 - i)) & 1)) << bit for i, bit in enumerate(bits))
        for place in range(1 << count)
    ]


def swap(values, axis, count, bit):
    return lax.ppermute(values, axis, [(i, i ^ (1 << bit)) for i in range(count)])


def outer_body(*refs, parts, offsets, size, direct, tables):
    own, refs = refs[0], refs[1:]
    lefts, rights, refs = refs[:parts[0]], refs[parts[0] : 2 * parts[0]], refs[2 * parts[0] :]
    held, out, scratch = refs[:tables], refs[tables], refs[tables + 1 :]
    start = 0
    rows = len(offsets) * size
    for number, (first, last) in enumerate(parts[1:]):
        left = lefts[number]
        if direct:
            picked = scratch[number]
            for place, offset in enumerate(offsets):
                source = pl.multiple_of((own[0] ^ offset) * size, 16)
                picked[place * size : (place + 1) * size, :] = left[pl.ds(source, size), :]
            left = picked
        wide = (last - first) * UNIT
        out[:rows, start : start + wide] = nn(left[...], rights[number][:, first * UNIT : last * UNIT])
        start += wide
    if tables:
        out[rows:, :] = jnp.zeros((out.shape[0] - rows, out.shape[1]), F32)
        place = rows
        line = held[0].shape[1]
        for table in held:
            for i in range(table.shape[0]):
                for at in range(0, table.shape[1], line):
                    out[place : place + 1, :line] = table[i : i + 1, at : at + line]
                    place += 1


EXTRA = 16


def fold_body(keep, recv, send_out, keep_out):
    half = keep_out.shape[0]
    send_out[...] = keep[:half, :] + recv[:half, :]
    keep_out[...] = keep[half:, :] + recv[half:, :]


def add_body(keep, recv, out):
    out[...] = keep[...] + recv[...]


def add_two_body(first, second, third, out):
    out[...] = first[...] + (second[...] + third[...])


def fold_extra_body(keep, recv, send_out, keep_out):
    half = keep_out.shape[0] - EXTRA
    tables = keep[2 * half :, :] + recv[2 * half :, :]
    send_out[:half, :] = keep[:half, :] + recv[:half, :]
    keep_out[:half, :] = keep[half : 2 * half, :] + recv[half : 2 * half, :]
    send_out[half:, :] = tables
    keep_out[half:, :] = tables


class Bag:
    pass


class Sums:
    def __init__(self, chain, own, count, sources):
        self.chain, self.own, self.count, self.sources = chain, own, count, sources
        self.steps, self.flying, self.held, self.done = {}, {}, {}, {}
        self.extra = {}

    def outer(self, name, which):
        letters, segments = PIECES[name]
        bits = bits_of(letters, self.count)
        order = block_order(bits)
        half = self.count // 2
        offsets = order[which * half : (which + 1) * half]
        lefts = [self.sources[source][0] for source, _, _ in segments]
        rights = [self.sources[source][1] for source, _, _ in segments]
        size = lefts[0].shape[0] // self.count
        direct = size % 16 == 0
        if not direct:
            blocks = self.own[0] ^ jnp.array(offsets, jnp.int32)
            lefts = [
                left.reshape(self.count, size, -1)[blocks].reshape(half * size, -1) for left in lefts
            ]
        tables = self.extra.get(name, [])
        rows = half * size + (EXTRA if tables else 0)
        wide = sum(last - first for _, first, last in segments) * UNIT
        volume = sum(left.size * 3 for left in lefts) + sum(right.size * 2 for right in rights) + rows * wide * 8
        return self.chain(
            functools.partial(
                outer_body,
                parts=(len(segments), *((first, last) for _, first, last in segments)),
                offsets=offsets,
                size=size,
                direct=direct,
                tables=len(tables),
            ),
            (self.own, *lefts, *rights, *tables),
            [SMEM] + [VMEM] * (2 * len(segments) + len(tables)),
            (shape((rows, wide)),),
            (VMEM,),
            8 + volume // MIB,
            "outer_" + name + str(which),
            scratch=[pltpu.VMEM((half * size, left.shape[1]), LOW) for left in lefts] if direct else [],
        )[0]

    def fly(self, name, values):
        step = self.steps.get(name, 0)
        bits = bits_of(PIECES[name][0], self.count)
        self.flying[name] = swap(values, DP, self.count, bits[step])
        self.steps[name] = step + 1

    def send(self, name):
        self.fly(name, self.outer(name, 0))

    def keep(self, name):
        self.held[name] = self.outer(name, 1)

    def fold(self, name):
        if name in self.done:
            return
        keep, recv = self.held[name], self.flying[name]
        more = EXTRA if name in self.extra else 0
        rows = keep.shape[0] - more
        wide = keep.shape[1]
        if self.steps[name] == self.count.bit_length() - 1:
            (self.done[name],) = self.chain(
                add_body,
                (keep, recv),
                [VMEM, VMEM],
                (shape(keep.shape),),
                (VMEM,),
                4 + (keep.size * 12) // MIB,
                "last_" + name,
            )
        elif rows % 32:
            total = keep + recv
            tables = total[rows:]
            self.held[name] = jnp.concatenate([total[rows // 2 : rows], tables])
            self.fly(name, jnp.concatenate([total[: rows // 2], tables]))
        else:
            first, self.held[name] = self.chain(
                fold_extra_body if more else fold_body,
                (keep, recv),
                [VMEM, VMEM],
                (shape((rows // 2 + more, wide)),) * 2,
                (VMEM, VMEM),
                4 + (keep.size * 14) // MIB,
                "fold_" + name + str(self.steps[name]),
            )
            self.fly(name, first)

    def finish(self):
        while len(self.done) < len(PIECES):
            for name in PIECES:
                self.fold(name)


PLAN = (
    "ffn", "S:b", "S:a", "cross", "K:c", "K:b", "S:c", "self", "turnx", "K:a", "K:e", "S:e", "F:a",
    "F:b", "S:d", "in", "F:c", "F:e", "F:a", "K:d", "F:b", "F:d", "F:c", "store", "F:e", "F:a", "F:b",
    "F:c", "rest", "F:e", "F:d", "F:b", "F:c", "F:d", "F:a", "F:e", "F:d",
)


def per_device(
    count,
    inputs,
    datastore,
    lengths,
    indices,
    w_query,
    b_query,
    w_key,
    w_value,
    b_value,
    w_out,
    b_out,
    g_one,
    c_one,
    wc_query,
    bc_query,
    wc_key,
    wc_value,
    bc_value,
    wc_out,
    bc_out,
    g_two,
    c_two,
    w_up,
    b_up,
    w_down,
    b_down,
    g_three,
    c_three,
    cotangent,
):
    x = inputs[0]
    memory = datastore[0]
    q_scale = 1.0 / math.sqrt(HD)
    rank = lax.axis_index(DP).astype(jnp.int32)
    own = rank.reshape(1)
    side = lax.axis_index(TENSOR).astype(jnp.int32).reshape(1)
    chain = Chain()
    sources = {}
    sums = Sums(chain, own, count, sources)

    def other_core(values):
        return lax.ppermute(values, TENSOR, [(0, 1), (1, 0)])

    q, k, v, probs, inverse, ot, attended, self_part = self_forward(
        chain, lengths, x, w_query, b_query, w_key, w_value, b_value, w_out
    )
    self_other = other_core(self_part)
    words = mask_words(chain, indices[0])
    keys, values_t = store_products(chain, memory, wc_key, wc_value, True)
    unit_one, inv_one, one_t, cross_query, cross_probs, cross_sums, cross_ot, context, cross_part = cross_forward(
        chain, x, self_part, self_other, b_out, g_one, c_one, wc_query, bc_query, words, keys, values_t, bc_value, wc_out
    )
    cross_other = other_core(cross_part)
    values, keys_t = store_products(chain, memory, wc_key, wc_value, False)
    unit_two, inv_two, two_t, hidden, slope, ffn_part = ffn_forward(
        chain, unit_one, g_one, c_one, cross_part, cross_other, bc_out, g_two, c_two, w_up, b_up, w_down
    )
    ffn_other = other_core(ffn_part)
    memory_t = turn(chain, memory)
    output, grad_three, grad_ffn, ffn_t, sums_three = norm_three(
        chain, unit_two, g_two, c_two, ffn_part, ffn_other, b_down, g_three, c_three, cotangent[0]
    )
    sources["down"] = (ffn_t, hidden)
    half = memory.shape[0] // 2
    rows, wide = x.shape
    cols = w_query.shape[1]
    g = Bag()

    def do_ffn():
        g.pre, g.sums_up, g.two_part = ffn_backward(chain, grad_ffn, w_down, slope, w_up)
        g.two_other = other_core(g.two_part)
        sources["up"] = (two_t, g.pre)

    def do_cross():
        g.two, cross_t, g.sums_two, g.sums_cross, g.keys, g.values, asked, g.one_part = cross_backward(
            chain, grad_three, g.two_part, g.two_other, unit_two, inv_two, g_two, wc_out, cross_ot, cross_sums,
            cross_probs, values, keys_t, cross_query, wc_query,
        )
        g.one_other = other_core(g.one_part)
        sources["key"] = (memory_t, g.keys)
        sources["value"] = (memory_t, g.values)
        sources["mix"] = (cross_t, context)
        sources["ask"] = (one_t, asked)

    def do_self():
        g.one, self_t, sums_one, sums_self, grad_q, grad_k, grad_v, g.in_part = self_backward(
            chain, g.two, g.one_part, g.one_other, unit_one, inv_one, g_one, w_out, ot, inverse, probs,
            q, k, v, w_query, w_key, w_value,
        )
        g.in_other = other_core(g.in_part)
        g.q, g.k, g.v = grad_q, grad_k, grad_v
        sources["out"] = (self_t, attended)
        sums.extra[EXTRA_PIECE] = [sums_three, g.sums_two, sums_one, sums_self, g.sums_cross, g.sums_up]

    def do_turn_x():
        x_t = turn(chain, x)
        sources["q"] = (x_t, g.q)
        sources["k"] = (x_t, g.k)
        sources["v"] = (x_t, g.v)

    def do_in():
        block = pl.BlockSpec((rows // 4, wide), lambda i: (i, 0))
        (g.input,) = chain(
            add_two_body,
            (g.one, g.in_part, g.in_other),
            [block] * 3,
            (shape((rows, wide)),),
            (block,),
            12,
            "input_sum",
            grid=4,
        )

    def do_store():
        (part,) = chain(
            functools.partial(store_term_body, flipped=True),
            (side, g.keys, g.values, wc_key, wc_value),
            [SMEM] + [VMEM] * 4,
            (shape((half, wide)),),
            (VMEM,),
            20,
            "store_other",
        )
        g.store_other = other_core(part)

    def do_rest():
        (g.store,) = chain(
            store_sum_body,
            (side, g.keys, g.values, wc_key, wc_value, g.store_other),
            [SMEM] + [VMEM] * 5,
            (shape((half, wide)),),
            (VMEM,),
            24,
            "store_own",
        )

    jobs = {"turnx": do_turn_x, "ffn": do_ffn, "cross": do_cross, "self": do_self, "in": do_in, "store": do_store, "rest": do_rest}
    verbs = {"S": sums.send, "K": sums.keep, "F": sums.fold}
    for step in PLAN:
        verb, _, name = step.partition(":")
        if name:
            verbs[verb](name)
        else:
            jobs[verb]()
    sums.finish()
    input_grad = g.input[None]
    datastore_grad = g.store

    found = {}
    for name, (_, segments) in PIECES.items():
        start = 0
        for source, first, last in segments:
            span = (last - first) * UNIT
            found.setdefault(source, []).append(sums.done[name][: wide // count, start : start + span])
            start += span
    found = {source: jnp.concatenate(blocks, axis=1) for source, blocks in found.items()}
    table = sums.done[EXTRA_PIECE][wide // count :, :wide]
    mine = lax.dynamic_slice_in_dim(table[:9], rank * (wide // count), wide // count, axis=1)
    pairs = table[9:11].reshape(4, cols)
    pairs = lax.dynamic_slice_in_dim(pairs, rank * (cols // count), cols // count, axis=1)
    ups = table[11 : 11 + w_up.shape[1] // wide].reshape(-1)
    grad_b_up = lax.dynamic_slice_in_dim(ups, rank * (ups.shape[0] // count), ups.shape[0] // count)
    return (
        output[None],
        input_grad,
        datastore_grad[None],
        found["q"] * q_scale,
        pairs[0],
        found["k"],
        found["v"],
        pairs[1],
        found["out"].T,
        mine[8],
        mine[6],
        mine[7],
        found["ask"] * q_scale,
        pairs[3],
        found["key"],
        found["value"],
        pairs[2],
        found["mix"].T,
        mine[5],
        mine[3],
        mine[4],
        found["up"],
        grad_b_up,
        found["down"].T,
        mine[2],
        mine[0],
        mine[1],
    )


def solution(mesh):
    return jax.shard_map(
        functools.partial(per_device, mesh.shape[DP]),
        mesh=mesh,
        in_specs=(
            P(DP, None, None),
            P(DP, None, None),
            P(DP),
            P(DP, None, None),
            P(None, TENSOR),
            P(TENSOR),
            P(None, TENSOR),
            P(None, TENSOR),
            P(TENSOR),
            P(TENSOR, None),
            P(),
            P(),
            P(),
            P(None, TENSOR),
            P(TENSOR),
            P(None, TENSOR),
            P(None, TENSOR),
            P(TENSOR),
            P(TENSOR, None),
            P(),
            P(),
            P(),
            P(None, TENSOR),
            P(TENSOR),
            P(TENSOR, None),
            P(),
            P(),
            P(),
            P(DP, None, None),
        ),
        out_specs=(
            P(DP, None, None),
            P(DP, None, None),
            P(DP, TENSOR, None),
            P(DP, TENSOR),
            P((TENSOR, DP)),
            P(DP, TENSOR),
            P(DP, TENSOR),
            P((TENSOR, DP)),
            P(TENSOR, DP),
            P(DP),
            P(DP),
            P(DP),
            P(DP, TENSOR),
            P((TENSOR, DP)),
            P(DP, TENSOR),
            P(DP, TENSOR),
            P((TENSOR, DP)),
            P(TENSOR, DP),
            P(DP),
            P(DP),
            P(DP),
            P(DP, TENSOR),
            P((TENSOR, DP)),
            P(TENSOR, DP),
            P(DP),
            P(DP),
            P(DP),
        ),
        check_vma=False,
    )
```

```python
import functools
import math

import jax
import jax.numpy as jnp
from jax import lax
from jax.experimental import pallas as pl
from jax.experimental.pallas import tpu as pltpu
from jax.sharding import PartitionSpec as P

HD = 64
NEG = -1e30
EPS = 1e-05
WORDS = 256
MIB = 1 << 20

F32 = jnp.float32
DP = "dp"
TENSOR = "tensor"
LOW = jnp.bfloat16


def nn(left, right):
    return lax.dot_general(left, right, (((1,), (0,)), ((), ())), preferred_element_type=F32)


def nt(left, right):
    return lax.dot_general(left, right, (((1,), (1,)), ((), ())), preferred_element_type=F32)


def tn(left, right):
    return lax.dot_general(left, right, (((0,), (0,)), ((), ())), preferred_element_type=F32)


def flip(values):
    return values.astype(F32).T


def row(ref):
    return ref[...].astype(F32).reshape(1, -1)


def spread_row(ref, out):
    values = row(ref)
    wide = out.shape[1]
    for i in range(out.shape[0]):
        out[i : i + 1, :] = values[:, i * wide : (i + 1) * wide]


def shape(dims, kind=F32):
    return jax.ShapeDtypeStruct(dims, kind)


VMEM = pl.BlockSpec(memory_space=pltpu.VMEM)
SMEM = pl.BlockSpec(memory_space=pltpu.SMEM)
ANY = pl.BlockSpec(memory_space=pl.ANY)


def whole(dims):
    return pl.BlockSpec(dims, lambda i: (0,) * len(dims), pipeline_mode=pl.Buffered(1))


def kept(dims):
    return pl.BlockSpec(dims, lambda i: (0,) * len(dims))


WEIGHTS = {"cross_b": 10000000000, "self_b": 1000000000, "fold_c": 1, "fold_b": 6000000000, "fold_d": 20000000000, "ffn_b": 6000000000, "outer": 10000000000, "fold": 40000000000, "": 1}


def weight_of(name):
    return next(weight for prefix, weight in WEIGHTS.items() if name.startswith(prefix))


class Chain:
    def __init__(self):
        self.token = None

    def __call__(self, body, args, ins, shapes, outs, mib, name, grid=None, scratch=()):
        given = len(args)
        extra = [] if self.token is None else [pltpu.with_memory_space_constraint(self.token, pltpu.HBM)]

        def kernel(*refs):
            refs = list(refs)
            token = refs.pop(given + len(extra) + len(shapes))
            del refs[given : given + len(extra)]
            body(*refs)
            token[...] = jnp.zeros_like(token)

        more = {} if grid is None else {"grid": (grid,)}
        args = [
            pltpu.with_memory_space_constraint(arg, pltpu.HBM) if spec.memory_space in (None, pl.ANY) else arg
            for arg, spec in zip(args, ins)
        ]
        shapes = [
            pltpu.HBM(out.shape, out.dtype) if spec.memory_space is None else out for out, spec in zip(shapes, outs)
        ]
        results = pl.pallas_call(
            kernel,
            out_shape=(*shapes, pltpu.HBM((8, 128), F32)),
            in_specs=[*ins, *([ANY] * len(extra))],
            out_specs=(*outs, whole((8, 128)) if grid else pl.BlockSpec((8, 128))),
            scratch_shapes=list(scratch),
            compiler_params=pltpu.CompilerParams(vmem_limit_bytes=mib * MIB),
            cost_estimate=pl.CostEstimate(flops=weight_of(name), bytes_accessed=1, transcendentals=0),
            name=name,
            **more,
        )(*args, *extra)
        self.token = results[-1]
        return results[:-1]


def norm_parts(values):
    average = jnp.mean(values, axis=-1, keepdims=True)
    centred = values - average
    variance = jnp.mean(centred * centred, axis=-1, keepdims=True)
    inverse = lax.rsqrt(variance + EPS)
    return centred * inverse, inverse


def norm_back(grad, gain, unit, inverse):
    scaled = grad * gain
    first = jnp.mean(scaled, axis=-1, keepdims=True)
    second = jnp.mean(scaled * unit, axis=-1, keepdims=True)
    return inverse * (scaled - first - unit * second)


def rows_of_half(values, half):
    place = lax.broadcasted_iota(jnp.int32, values.shape, 0)
    return jnp.where((place // HD) == half, values, jnp.zeros_like(values))


def lanes_of_half(values, half):
    place = lax.broadcasted_iota(jnp.int32, values.shape, 1)
    return jnp.where((place // HD) == half, values, jnp.zeros_like(values))


def self_forward_body(
    length, x, wq, bq, wk, wv, bv, wo,
    q_out, k_out, v_out, p_out, inv_out, ot_out, att_out, part_out,
    bias, q_low, k_low, v_low, probs, done,
):
    rows = x.shape[0]
    heads = wq.shape[1] // HD
    q_scale = 1.0 / math.sqrt(HD)
    copies = []

    def leave(source, target):
        copy = pltpu.make_async_copy(source, target, done.at[len(copies)])
        copy.start()
        copies.append(copy)

    x_low = x[...]
    q = ((nn(x_low, wq[...]) + row(bq)) * q_scale).astype(LOW)
    k = nn(x_low, wk[...]).astype(LOW)
    v = (nn(x_low, wv[...]) + row(bv)).astype(LOW)
    q_low[...] = q
    k_low[...] = k
    v_low[...] = v
    leave(q_low, q_out)
    leave(k_low, k_out)
    leave(v_low, v_out)
    qt = flip(q).astype(LOW)
    vt = flip(v).astype(LOW)
    key = lax.broadcasted_iota(jnp.int32, (rows, rows), 0)
    query = lax.broadcasted_iota(jnp.int32, (rows, rows), 1)
    bias[...] = jnp.where((key <= query) & (key < length[0]), 0.0, NEG)
    for head in range(heads):
        pair, half = head // 2, head % 2
        lanes = slice(pair * 2 * HD, (pair + 1) * 2 * HD)
        own = slice(head * HD, (head + 1) * HD)
        scores = nn(k[:, lanes], rows_of_half(qt[lanes], half)) + bias[...]
        top = jnp.max(scores, axis=0, keepdims=True)
        grown = jnp.exp(scores - top)
        inverse = 1.0 / jnp.sum(grown, axis=0, keepdims=True)
        low = grown.astype(LOW)
        probs[head] = low
        leave(probs.at[head], p_out.at[head])
        inv_out[pair, half : half + 1, :] = inverse
        ot_out[own, :] = nn(vt[own], low) * inverse
    attended = ot_out[...].T.astype(LOW)
    att_out[...] = attended
    part_out[...] = nn(attended, wo[...])
    for copy in copies:
        copy.wait()


def self_forward(chain, length, x, wq, bq, wk, wv, bv, wo):
    rows, width = x.shape
    cols = wq.shape[1]
    heads = cols // HD
    pairs = heads // 2
    side = whole((width, cols))
    return chain(
        self_forward_body,
        (length, x, wq, bq, wk, wv, bv, wo),
        [SMEM, whole((rows, width)), side, whole((cols,)), side, side, whole((cols,)), whole((cols, width))],
        (
            pltpu.HBM((rows, cols), LOW),
            pltpu.HBM((rows, cols), LOW),
            pltpu.HBM((rows, cols), LOW),
            pltpu.HBM((heads, rows, rows), LOW),
            shape((pairs, 2, rows)),
            shape((cols, rows)),
            shape((rows, cols), LOW),
            shape((rows, width)),
        ),
        (
            ANY, ANY, ANY, ANY,
            whole((pairs, 2, rows)),
            whole((cols, rows)),
            whole((rows, cols)),
            VMEM,
        ),
        28,
        "self_forward",
        grid=1,
        scratch=[
            pltpu.VMEM((rows, rows), F32),
            pltpu.VMEM((rows, cols), LOW),
            pltpu.VMEM((rows, cols), LOW),
            pltpu.VMEM((rows, cols), LOW),
            pltpu.VMEM((heads, rows, rows), LOW),
            pltpu.SemaphoreType.DMA((heads + 3,)),
        ],
    )


def mask_body(picks, words, sums):
    step = pl.program_id(0)
    block = picks.shape[0]
    up = lax.broadcasted_iota(jnp.int32, (256, 256), 0)
    across = lax.broadcasted_iota(jnp.int32, (256, 256), 1)
    same = (up & 15) == (across & 15)
    for part in range(block // 16):
        index = picks[part * 16 : (part + 1) * 16, :]
        bit = lax.shift_left(jnp.ones_like(index), index >> 8).astype(F32).astype(LOW)
        upper = ((index >> 4) & 15).astype(F32).astype(LOW)
        lower = (index & 15).astype(F32).astype(LOW)
        zero = jnp.zeros_like(bit)
        one = jnp.ones_like(bit)
        left = jnp.concatenate([jnp.where(upper == c, bit, zero) for c in range(16)], axis=0)
        right = jnp.concatenate([jnp.where(lower == c, one, zero) for c in range(16)], axis=0)
        cross = jnp.where(same, nt(left, right), 0.0).astype(LOW)
        start = pl.multiple_of(step * block + part * 16, 16)
        for c in range(16):
            sums[pl.ds(start, 16), c * 256 : (c + 1) * 256] = cross[c * 16 : (c + 1) * 16, :]

    @pl.when(step == pl.num_programs(0) - 1)
    def _():
        word = lax.broadcasted_iota(jnp.int32, (256, 4096), 0)
        place = lax.broadcasted_iota(jnp.int32, (256, 4096), 1)
        fold = jnp.where((place >> 4) == word, 1.0, 0.0).astype(LOW)
        words[...] = nt(fold, sums[...]).astype(jnp.int32)


def mask_words(chain, picks):
    rows, chosen = picks.shape
    block = math.gcd(rows, 256)
    return chain(
        mask_body,
        (picks,),
        [pl.BlockSpec((block, chosen), lambda i: (i, 0))],
        (shape((WORDS, rows), jnp.int32),),
        (whole((WORDS, rows)),),
        28,
        "mask_words",
        grid=rows // block,
        scratch=[pltpu.VMEM((rows, 16 * 256), LOW)],
    )[0]


def put_pairs(out, values):
    high = values.astype(LOW)
    rest = (values - high.astype(F32)).astype(LOW)
    pair = 2 * HD
    for i in range(values.shape[1] // pair):
        out[:, 2 * i * pair : (2 * i + 1) * pair] = high[:, i * pair : (i + 1) * pair]
        out[:, (2 * i + 1) * pair : (2 * i + 2) * pair] = rest[:, i * pair : (i + 1) * pair]


def put_heads(out, values):
    high = values.astype(LOW)
    rest = (values - high.astype(F32)).astype(LOW)
    for i in range(values.shape[0] // HD):
        out[2 * i * HD : (2 * i + 1) * HD, :] = high[i * HD : (i + 1) * HD, :]
        out[(2 * i + 1) * HD : (2 * i + 2) * HD, :] = rest[i * HD : (i + 1) * HD, :]


def store_body(memory, wk, wv, k_out, vt_out):
    low = memory[...]
    put_pairs(k_out, nn(low, wk[...]))
    turned = (((0,), (1,)), ((), ()))
    put_heads(vt_out, lax.dot_general(wv[...], low, turned, preferred_element_type=F32))


def store_turned_body(memory, wk, wv, v_out, kt_out):
    low = memory[...]
    put_pairs(v_out, nn(low, wv[...]))
    turned = (((0,), (1,)), ((), ()))
    put_heads(kt_out, lax.dot_general(wk[...], low, turned, preferred_element_type=F32))


def store_products(chain, memory, wk, wv, first):
    entries, width = memory.shape
    cols = wk.shape[1]
    block = 1024
    return chain(
        store_body if first else store_turned_body,
        (memory, wk, wv),
        [pl.BlockSpec((block, width), lambda i: (i, 0)), whole((width, cols)), whole((width, cols))],
        (shape((entries, 2 * cols), LOW), shape((2 * cols, entries), LOW)),
        (pl.BlockSpec((block, 2 * cols), lambda i: (i, 0)), pl.BlockSpec((2 * cols, block), lambda i: (0, i))),
        32,
        "store_products" if first else "store_turned",
        grid=entries // block,
    )


def cross_forward_body(
    x, own, other, b_out, g_one, c_one, wq, bq, words, keys, values_t, bv, wo,
    unit_out, inv_out, turn_out, q_out, p_out, sum_out, ot_out, ctx_out, part_out,
    qt, bias, scores, keys_held, values_held, probs, loads, leaves,
):
    q_scale = 1.0 / math.sqrt(HD)
    entries = keys.shape[0]
    heads = wq.shape[1] // HD
    chunk = 512
    wide = 4 * HD

    def load(pair):
        lanes = pl.ds(pl.multiple_of(pair * wide, wide), wide)
        return (
            pltpu.make_async_copy(keys.at[:, lanes], keys_held.at[pair], loads.at[0, pair]),
            pltpu.make_async_copy(values_t.at[lanes, :], values_held.at[pair], loads.at[1, pair]),
        )

    def leave(pair, half):
        return pltpu.make_async_copy(probs.at[half], p_out.at[2 * pair + half], leaves.at[half])

    for pair in range(heads // 2):
        for copy in load(pair):
            copy.start()
    total = x[...].astype(F32) + (own[...] + other[...] + row(b_out))
    unit, inverse = norm_parts(total)
    unit_out[...] = unit
    inv_out[...] = inverse
    low = (unit * row(g_one) + row(c_one)).astype(LOW)
    turn_out[...] = flip(low).astype(LOW)
    q = ((nn(low, wq[...]) + row(bq)) * q_scale).astype(LOW)
    q_out[...] = q
    qt[...] = flip(q).astype(LOW)
    held = words[...]
    for part in range(entries // WORDS):
        bias[part * WORDS : (part + 1) * WORDS, :] = jnp.where(((held >> part) & 1) == 1, 0.0, NEG)

    def one_pair(pair, carry):
        for copy in load(pair):
            copy.wait()
        pair_rows = qt[pl.ds(pl.multiple_of(pair * 2 * HD, 2 * HD), 2 * HD), :]
        for half in range(2):
            query = rows_of_half(pair_rows, half)
            query = jnp.concatenate([query, query], axis=0)
            top = None
            for part in range(entries // chunk):
                span = slice(part * chunk, (part + 1) * chunk)
                piece = nn(keys_held[pair, span, :], query) + bias[span, :]
                scores[half, span, :] = piece
                peak = jnp.max(piece.reshape(chunk // 8, 8, -1), axis=0)
                top = peak if top is None else jnp.maximum(top, peak)
            top = jnp.max(top, axis=0, keepdims=True)

            @pl.when(pair > 0)
            def _():
                leave(pair - 1, half).wait()

            total = pooled = None
            for part in range(entries // chunk):
                span = slice(part * chunk, (part + 1) * chunk)
                grown = jnp.exp(scores[half, span, :] - top)
                low = grown.astype(LOW)
                probs[half, span, :] = low
                mass = jnp.sum(grown.reshape(chunk // 8, 8, -1), axis=0)
                term = nn(values_held[pair, half * 2 * HD : (half + 1) * 2 * HD, span], low)
                total, pooled = (mass, term) if total is None else (total + mass, pooled + term)
            leave(pair, half).start()
            inverse = 1.0 / jnp.sum(total, axis=0, keepdims=True)
            head = 2 * pair + half
            sum_out[pl.ds(head, 1), :] = inverse
            ot_out[pl.ds(pl.multiple_of(head * HD, HD), HD), :] = (pooled[:HD] + pooled[HD:]) * inverse
        return carry

    lax.fori_loop(0, heads // 2, one_pair, 0)
    context = (ot_out[...].T + row(bv)).astype(LOW)
    ctx_out[...] = context
    part_out[...] = nn(context, wo[...])
    for half in range(2):
        leave(heads // 2 - 1, half).wait()


def cross_forward(chain, x, own, other, b_out, g_one, c_one, wq, bq, words, keys, values_t, bv, wo):
    rows, width = x.shape
    entries = keys.shape[0]
    cols = wq.shape[1]
    heads = cols // HD
    line = whole((width,))
    thin = whole((cols,))
    return chain(
        cross_forward_body,
        (x, own, other, b_out, g_one, c_one, wq, bq, words, keys, values_t, bv, wo),
        [whole((rows, width)), VMEM, VMEM, line, line, line, whole((width, cols)), thin, whole((WORDS, rows)),
         ANY, ANY, thin, whole((cols, width))],
        (
            shape((rows, width)),
            shape((rows, 1)),
            shape((width, rows), LOW),
            shape((rows, cols), LOW),
            pltpu.HBM((heads, entries, rows), LOW),
            shape((heads, rows)),
            shape((cols, rows)),
            shape((rows, cols), LOW),
            shape((rows, width)),
        ),
        (VMEM, whole((rows, 1)), VMEM, VMEM, ANY, VMEM, whole((cols, rows)), VMEM, VMEM),
        38,
        "cross_forward",
        grid=1,
        scratch=[
            pltpu.VMEM((cols, rows), LOW),
            pltpu.VMEM((entries, rows), F32),
            pltpu.VMEM((2, entries, rows), F32),
            pltpu.VMEM((heads // 2, entries, 4 * HD), LOW),
            pltpu.VMEM((heads // 2, 4 * HD, entries), LOW),
            pltpu.VMEM((2, entries, rows), LOW),
            pltpu.SemaphoreType.DMA((2, heads // 2)),
            pltpu.SemaphoreType.DMA((2,)),
        ],
    )


def ffn_forward_body(
    unit_one, g_one, c_one, own, other, b_out, g_two, c_two, w_up, b_up, w_down,
    unit_out, inv_out, turn_out, hid_out, slope_out, part_out, low_two, bias,
):
    step = pl.program_id(0)

    @pl.when(step == 0)
    def _():
        total = unit_one[...] * row(g_one) + row(c_one) + (own[...] + other[...] + row(b_out))
        unit, inverse = norm_parts(total)
        unit_out[...] = unit
        inv_out[...] = inverse
        low = (unit * row(g_two) + row(c_two)).astype(LOW)
        low_two[...] = low
        spread_row(b_up, bias)
        turn_out[...] = flip(low).astype(LOW)

    pre = nn(low_two[...], w_up[...]) + bias[pl.ds(step, 1), :]
    below = 0.5 * (1.0 + lax.erf(pre * math.sqrt(0.5)))
    density = jnp.exp(-0.5 * pre * pre) * (1.0 / math.sqrt(2.0 * math.pi))
    lanes = pl.ds(pl.multiple_of(step * pre.shape[1], pre.shape[1]), pre.shape[1])
    slope_out[...] = below + pre * density
    hidden = (pre * below).astype(LOW)
    hid_out[:, lanes] = hidden
    term = nn(hidden, w_down[...])

    @pl.when(step == 0)
    def _():
        part_out[...] = term

    @pl.when(step > 0)
    def _():
        part_out[...] += term


def ffn_forward(chain, unit_one, g_one, c_one, own, other, b_out, g_two, c_two, w_up, b_up, w_down):
    rows, width = unit_one.shape
    units = w_up.shape[1]
    block = 768
    return chain(
        ffn_forward_body,
        (unit_one, g_one, c_one, own, other, b_out, g_two, c_two, w_up, b_up, w_down),
        [
            VMEM,
            whole((width,)),
            whole((width,)),
            VMEM,
            VMEM,
            whole((width,)),
            whole((width,)),
            whole((width,)),
            pl.BlockSpec((width, block), lambda i: (0, i)),
            whole((units,)),
            pl.BlockSpec((block, width), lambda i: (i, 0)),
        ],
        (
            shape((rows, width)),
            shape((rows, 1)),
            shape((width, rows), LOW),
            shape((rows, units), LOW),
            shape((rows, units)),
            shape((rows, width)),
        ),
        (VMEM, whole((rows, 1)), whole((width, rows)), VMEM, pl.BlockSpec((rows, block), lambda i: (0, i)), VMEM),
        30,
        "ffn_forward",
        grid=units // block,
        scratch=[pltpu.VMEM((rows, width), LOW), pltpu.VMEM((units // block, block), F32)],
    )


def norm_three_body(unit_two, g_two, c_two, own, other, b_down, g_three, c_three, cotangent, out, grad, low, turn, sums):
    step = pl.program_id(0)
    block = out.shape[0]
    span = pl.ds(pl.multiple_of(step * block, block), block)
    total = unit_two[span, :] * row(g_two) + row(c_two) + (own[span, :] + other[span, :] + row(b_down))
    unit, inverse = norm_parts(total)
    out[...] = (unit * row(g_three) + row(c_three)).astype(LOW)
    seed = cotangent[...].astype(F32)
    back = norm_back(seed, row(g_three), unit, inverse)
    rounded = back.astype(LOW)
    grad[span, :] = back
    low[span, :] = rounded
    turn[:, span] = flip(rounded).astype(LOW)

    @pl.when(step == 0)
    def _():
        sums[...] = jnp.zeros_like(sums)

    sums[0:1, :] += jnp.sum(seed * unit, axis=0, keepdims=True)
    sums[1:2, :] += jnp.sum(seed, axis=0, keepdims=True)
    sums[2:3, :] += jnp.sum(rounded.astype(F32), axis=0, keepdims=True)


def norm_three(chain, *args):
    rows, width = args[0].shape
    block = rows // 2
    tall = pl.BlockSpec((block, width), lambda i: (i, 0))
    line = whole((width,))
    return chain(
        norm_three_body,
        args,
        [VMEM, line, line, VMEM, VMEM, line, line, line, tall],
        (
            shape((rows, width), LOW),
            shape((rows, width)),
            shape((rows, width), LOW),
            shape((width, rows), LOW),
            shape((3, width)),
        ),
        (tall, VMEM, VMEM, VMEM, VMEM),
        12,
        "norm_three",
        grid=2,
    )


def ffn_backward_body(grad, w_down, slope, w_up, pre_out, sum_out, part_out):
    step = pl.program_id(0)
    block = w_down.shape[0]
    lanes = pl.ds(pl.multiple_of(step * block, block), block)
    back = (nt(grad[...], w_down[...]) * slope[...]).astype(LOW)
    pre_out[:, lanes] = back
    sum_out[:, lanes] = jnp.sum(back.astype(F32), axis=0, keepdims=True)
    term = nt(back, w_up[...])

    @pl.when(step == 0)
    def _():
        part_out[...] = term

    @pl.when(step > 0)
    def _():
        part_out[...] += term


def ffn_backward(chain, grad, w_down, slope, w_up):
    rows, width = grad.shape
    units = w_up.shape[1]
    block = 768
    return chain(
        ffn_backward_body,
        (grad, w_down, slope, w_up),
        [
            VMEM,
            pl.BlockSpec((block, width), lambda i: (i, 0)),
            pl.BlockSpec((rows, block), lambda i: (0, i)),
            pl.BlockSpec((width, block), lambda i: (0, i)),
        ],
        (shape((rows, units), LOW), shape((1, units)), shape((rows, width))),
        (VMEM, whole((1, units)), VMEM),
        26,
        "ffn_backward",
        grid=units // block,
    )


def cross_backward_body(
    grad_three, own, other, unit_two, inv_two, g_two, wo, ot, sums, probs, values, keys_t, query, wq,
    grad_out, turn_out, norm_sums, head_sums, dk_out, dv_out, dq_out, part_out,
    dctx_t, dq_t, change, grad_held, probs_held, values_held, keys_held, loads, brings, done,
):
    q_scale = 1.0 / math.sqrt(HD)
    entries = values.shape[0]
    cols = wq.shape[1]
    heads = cols // HD
    chunk = 512
    wide = 4 * HD

    def load(pair):
        lanes = pl.ds(pl.multiple_of(pair * wide, wide), wide)
        return (
            pltpu.make_async_copy(values.at[:, lanes], values_held.at[pair], loads.at[0, pair]),
            pltpu.make_async_copy(keys_t.at[lanes, :], keys_held.at[pair], loads.at[1, pair]),
        )

    def bring(pair, half):
        return pltpu.make_async_copy(probs.at[2 * pair + half], probs_held.at[half], brings.at[half])

    bring(0, 0).start()
    for pair in range(heads // 2):
        for copy in load(pair):
            copy.start()
        if pair == 0:
            bring(0, 1).start()
    grad_in = grad_three[...] + (own[...] + other[...])
    unit = unit_two[...]
    grad = norm_back(grad_in, row(g_two), unit, inv_two[...])
    grad_held[...] = grad
    keep = pltpu.make_async_copy(grad_held, grad_out, done)
    keep.start()
    low = grad.astype(LOW)
    turn_out[...] = flip(low).astype(LOW)
    norm_sums[0:1, :] = jnp.sum(grad_in * unit, axis=0, keepdims=True)
    norm_sums[1:2, :] = jnp.sum(grad_in, axis=0, keepdims=True)
    norm_sums[2:3, :] = jnp.sum(low.astype(F32), axis=0, keepdims=True)
    dctx_t[...] = nt(wo[...], low)
    head_sums[0:1, :cols] = jnp.sum(dctx_t[...].T, axis=0, keepdims=True)

    def one_pair(pair, carry):
        for copy in load(pair):
            copy.wait()
        lanes = pl.ds(pl.multiple_of(pair * 2 * HD, 2 * HD), 2 * HD)
        pair_query = query[:, lanes]
        for half in range(2):
            head = 2 * pair + half
            own_rows = pl.ds(pl.multiple_of(head * HD, HD), HD)
            scaled = (dctx_t[own_rows, :] * sums[pl.ds(head, 1), :]).astype(LOW)
            inner = jnp.sum(scaled.astype(F32) * ot[own_rows, :], axis=0, keepdims=True)
            empty = jnp.zeros_like(scaled)
            grad_rows = jnp.concatenate([scaled, empty] if half == 0 else [empty, scaled], axis=0)
            own_grad = flip(grad_rows).astype(LOW)
            grad_rows = jnp.concatenate([grad_rows, grad_rows], axis=0)
            own_query = lanes_of_half(pair_query, half)
            bring(pair, half).wait()
            for part in range(entries // chunk):
                span = slice(part * chunk, (part + 1) * chunk)
                low_probs = probs_held[half, span, :]
                shift = nn(values_held[pair, span, :], grad_rows) - inner
                delta = (low_probs.astype(F32) * shift).astype(LOW)
                change[half, span, :] = delta
                k_term = nn(delta, own_query).astype(LOW)
                v_term = nn(low_probs, own_grad).astype(LOW)
                if half == 0:
                    dk_out[span, lanes] = k_term
                    dv_out[span, lanes] = v_term
                else:
                    dk_out[span, lanes] = dk_out[span, lanes] + k_term
                    dv_out[span, lanes] = dv_out[span, lanes] + v_term

            @pl.when(pair + 1 < heads // 2)
            def _():
                bring(pair + 1, half).start()

            both = nn(keys_held[pair, half * 2 * HD : (half + 1) * 2 * HD, :], change[half])
            dq_t[own_rows, :] = both[:HD] + both[HD:]
        return carry

    lax.fori_loop(0, heads // 2, one_pair, 0)
    dq = dq_t[...].T.astype(LOW)
    dq_out[...] = dq
    head_sums[0:1, cols:] = jnp.sum(dq.astype(F32), axis=0, keepdims=True) * q_scale
    part_out[...] = nt(dq, wq[...]) * q_scale
    keep.wait()


def cross_backward(chain, *args):
    rows, width = args[0].shape
    entries = args[10].shape[0]
    cols = args[13].shape[1]
    heads = cols // HD
    return chain(
        cross_backward_body,
        args,
        [VMEM, VMEM, VMEM, VMEM, whole((rows, 1)), whole((width,)), whole((cols, width)), whole((cols, rows)), VMEM,
         ANY, ANY, ANY, VMEM, whole((width, cols))],
        (
            pltpu.HBM((rows, width), F32),
            shape((width, rows), LOW),
            shape((3, width)),
            shape((1, 2 * cols)),
            shape((entries, cols), LOW),
            shape((entries, cols), LOW),
            shape((rows, cols), LOW),
            shape((rows, width)),
        ),
        (ANY, VMEM, whole((3, width)), whole((1, 2 * cols)), VMEM, VMEM, VMEM, VMEM),
        32,
        "cross_backward",
        grid=1,
        scratch=[
            pltpu.VMEM((cols, rows), F32),
            pltpu.VMEM((cols, rows), F32),
            pltpu.VMEM((2, entries, rows), LOW),
            pltpu.VMEM((rows, width), F32),
            pltpu.VMEM((2, entries, rows), LOW),
            pltpu.VMEM((heads // 2, entries, 4 * HD), LOW),
            pltpu.VMEM((heads // 2, 4 * HD, entries), LOW),
            pltpu.SemaphoreType.DMA((2, heads // 2)),
            pltpu.SemaphoreType.DMA((2,)),
            pltpu.SemaphoreType.DMA,
        ],
    )


def self_backward_body(
    grad_two, own, other, unit_one, inv_one, g_one, wo, ot, inverse, probs, q, k, v, wq, wk, wv,
    grad_out, turn_out, norm_sums, head_sums, dq_out, dk_out, dv_out, part_out,
    datt_t, grad_held, done,
):
    step = pl.program_id(0)
    q_scale = 1.0 / math.sqrt(HD)
    cols = datt_t.shape[0]

    @pl.when(step == 0)
    def _():
        grad_in = grad_two[...] + (own[...] + other[...])
        unit = unit_one[...]
        grad = norm_back(grad_in, row(g_one), unit, inv_one[...])
        grad_held[...] = grad
        pltpu.make_async_copy(grad_held, grad_out, done).start()
        low = grad.astype(LOW)
        turn_out[...] = flip(low).astype(LOW)
        norm_sums[0:1, :] = jnp.sum(grad_in * unit, axis=0, keepdims=True)
        norm_sums[1:2, :] = jnp.sum(grad_in, axis=0, keepdims=True)
        norm_sums[2:3, :] = jnp.sum(low.astype(F32), axis=0, keepdims=True)
        datt_t[...] = nt(wo[...], low)

    pair_grad = datt_t[pl.ds(pl.multiple_of(step * 2 * HD, 2 * HD), 2 * HD), :]
    place = lax.broadcasted_iota(jnp.int32, pair_grad.shape, 0)
    scaled = pair_grad * jnp.where(place < HD, inverse[0, 0:1, :], inverse[0, 1:2, :])
    scaled_low = scaled.astype(LOW)
    weighed = scaled_low.astype(F32) * ot[...]
    scaled_rows = flip(scaled_low).astype(LOW)
    pair_query = q[...]
    pair_values = v[...]
    keys_t = flip(k[...]).astype(LOW)
    dk = None
    dv = None
    dq_t = []
    for half in range(2):
        inner = jnp.sum(weighed[half * HD : (half + 1) * HD, :], axis=0, keepdims=True)
        low_probs = probs[half]
        shift = nn(pair_values, rows_of_half(scaled_low, half)) - inner
        delta = (low_probs.astype(F32) * shift).astype(LOW)
        k_term = nn(delta, lanes_of_half(pair_query, half))
        v_term = nn(low_probs, lanes_of_half(scaled_rows, half))
        dk = k_term if dk is None else dk + k_term
        dv = v_term if dv is None else dv + v_term
        dq_t.append(nn(keys_t[half * HD : (half + 1) * HD], delta))
    dq = jnp.concatenate(dq_t, axis=0).T.astype(LOW)
    dk_low = dk.astype(LOW)
    dv_low = dv.astype(LOW)
    lanes = pl.ds(pl.multiple_of(step * 2 * HD, 2 * HD), 2 * HD)
    dq_out[:, lanes] = dq
    dk_out[:, lanes] = dk_low
    dv_out[:, lanes] = dv_low
    later = pl.ds(pl.multiple_of(cols + step * 2 * HD, 2 * HD), 2 * HD)
    head_sums[0:1, lanes] = jnp.sum(dq.astype(F32), axis=0, keepdims=True) * q_scale
    head_sums[0:1, later] = jnp.sum(dv_low.astype(F32), axis=0, keepdims=True)
    term = nt(dq, wq[...]) * q_scale + nt(
        jnp.concatenate([dk_low, dv_low], axis=1), jnp.concatenate([wk[...], wv[...]], axis=1)
    )

    @pl.when(step == 0)
    def _():
        part_out[...] = term

    @pl.when(step > 0)
    def _():
        part_out[...] += term

    @pl.when(step == pl.num_programs(0) - 1)
    def _():
        pltpu.make_async_copy(grad_held, grad_out, done).wait()


def self_backward(chain, *args):
    rows, width = args[0].shape
    cols = args[10].shape[1]
    pairs = cols // (2 * HD)
    tall = pl.BlockSpec((rows, 2 * HD), lambda i: (0, i))
    side = pl.BlockSpec((width, 2 * HD), lambda i: (0, i))
    return chain(
        self_backward_body,
        args,
        [
            whole((rows, width)),
            VMEM,
            VMEM,
            whole((rows, width)),
            whole((rows, 1)),
            whole((width,)),
            whole((cols, width)),
            pl.BlockSpec((2 * HD, rows), lambda i: (i, 0)),
            pl.BlockSpec((1, 2, rows), lambda i: (i, 0, 0)),
            pl.BlockSpec((2, rows, rows), lambda i: (i, 0, 0)),
            tall, tall, tall, side, side, side,
        ],
        (
            pltpu.HBM((rows, width), F32),
            shape((width, rows), LOW),
            shape((3, width)),
            shape((1, 2 * cols)),
            shape((rows, cols), LOW),
            shape((rows, cols), LOW),
            shape((rows, cols), LOW),
            shape((rows, width)),
        ),
        (ANY, VMEM, whole((3, width)), whole((1, 2 * cols)), VMEM, VMEM, VMEM, VMEM),
        18,
        "self_backward",
        grid=pairs,
        scratch=[pltpu.VMEM((cols, rows), F32), pltpu.VMEM((rows, width), F32), pltpu.SemaphoreType.DMA],
    )


def store_term_body(side, keys, values, wk, wv, out, *, flipped):
    rows = out.shape[0]
    which = 1 - side[0] if flipped else side[0]
    span = pl.ds(pl.multiple_of(which * rows, rows), rows)
    out[...] = nt(keys[span, :], wk[...]) + nt(values[span, :], wv[...])


def store_sum_body(side, keys, values, wk, wv, other, out):
    store_term_body(side, keys, values, wk, wv, out, flipped=False)
    out[...] += other[...]


def turn_body(values, out):
    out[...] = flip(values[...]).astype(LOW)


def turn(chain, values):
    rows, width = values.shape
    block = min(rows, 1024)
    return chain(
        turn_body,
        (values,),
        [pl.BlockSpec((block, width), lambda i: (i, 0))],
        (shape((width, rows), LOW),),
        (pl.BlockSpec((width, block), lambda i: (0, i)),),
        28,
        "turn",
        grid=rows // block,
    )[0]


BITS = {"x": 0, "y": 1, "l": 2, "h": 3}

PIECES = {
    "a": ("lhxy", (("down", 0, 11),)),
    "b": ("xlyh", (("down", 11, 12), ("up", 0, 12))),
    "c": ("yxlh", (("key", 0, 3), ("value", 0, 3), ("mix", 0, 3), ("ask", 0, 3))),
    "d": ("yxlh", (("q", 0, 3), ("k", 0, 3))),
    "e": ("xlyh", (("v", 0, 3), ("out", 0, 3))),
}
EXTRA_PIECE = "d"
UNIT = 128


def bits_of(letters, count):
    total = count.bit_length() - 1
    chosen = [BITS[letter] for letter in letters if BITS[letter] < total]
    return chosen + [bit for bit in range(total) if bit not in chosen]


def block_order(bits):
    count = len(bits)
    return [
        sum((1 - ((place >> (count - 1 - i)) & 1)) << bit for i, bit in enumerate(bits))
        for place in range(1 << count)
    ]


def swap(values, axis, count, bit):
    return lax.ppermute(values, axis, [(i, i ^ (1 << bit)) for i in range(count)])


def outer_body(*refs, parts, offsets, size, direct, tables):
    own, refs = refs[0], refs[1:]
    lefts, rights, refs = refs[:parts[0]], refs[parts[0] : 2 * parts[0]], refs[2 * parts[0] :]
    held, out, scratch = refs[:tables], refs[tables], refs[tables + 1 :]
    start = 0
    rows = len(offsets) * size
    for number, (first, last) in enumerate(parts[1:]):
        left = lefts[number]
        if direct:
            picked = scratch[number]
            for place, offset in enumerate(offsets):
                source = pl.multiple_of((own[0] ^ offset) * size, 16)
                picked[place * size : (place + 1) * size, :] = left[pl.ds(source, size), :]
            left = picked
        wide = (last - first) * UNIT
        out[:rows, start : start + wide] = nn(left[...], rights[number][:, first * UNIT : last * UNIT])
        start += wide
    if tables:
        out[rows:, :] = jnp.zeros((out.shape[0] - rows, out.shape[1]), F32)
        place = rows
        line = held[0].shape[1]
        for table in held:
            for i in range(table.shape[0]):
                for at in range(0, table.shape[1], line):
                    out[place : place + 1, :line] = table[i : i + 1, at : at + line]
                    place += 1


EXTRA = 16


def fold_body(keep, recv, send_out, keep_out):
    half = keep_out.shape[0]
    send_out[...] = keep[:half, :] + recv[:half, :]
    keep_out[...] = keep[half:, :] + recv[half:, :]


def add_body(keep, recv, out):
    out[...] = keep[...] + recv[...]


def add_two_body(first, second, third, out):
    out[...] = first[...] + (second[...] + third[...])


def fold_extra_body(keep, recv, send_out, keep_out):
    half = keep_out.shape[0] - EXTRA
    tables = keep[2 * half :, :] + recv[2 * half :, :]
    send_out[:half, :] = keep[:half, :] + recv[:half, :]
    keep_out[:half, :] = keep[half : 2 * half, :] + recv[half : 2 * half, :]
    send_out[half:, :] = tables
    keep_out[half:, :] = tables


class Bag:
    pass


class Sums:
    def __init__(self, chain, own, count, sources):
        self.chain, self.own, self.count, self.sources = chain, own, count, sources
        self.steps, self.flying, self.held, self.done = {}, {}, {}, {}
        self.extra = {}

    def outer(self, name, which):
        letters, segments = PIECES[name]
        bits = bits_of(letters, self.count)
        order = block_order(bits)
        half = self.count // 2
        offsets = order[which * half : (which + 1) * half]
        lefts = [self.sources[source][0] for source, _, _ in segments]
        rights = [self.sources[source][1] for source, _, _ in segments]
        size = lefts[0].shape[0] // self.count
        direct = size % 16 == 0
        if not direct:
            blocks = self.own[0] ^ jnp.array(offsets, jnp.int32)
            lefts = [
                left.reshape(self.count, size, -1)[blocks].reshape(half * size, -1) for left in lefts
            ]
        tables = self.extra.get(name, [])
        rows = half * size + (EXTRA if tables else 0)
        wide = sum(last - first for _, first, last in segments) * UNIT
        volume = sum(left.size * 3 for left in lefts) + sum(right.size * 2 for right in rights) + rows * wide * 8
        return self.chain(
            functools.partial(
                outer_body,
                parts=(len(segments), *((first, last) for _, first, last in segments)),
                offsets=offsets,
                size=size,
                direct=direct,
                tables=len(tables),
            ),
            (self.own, *lefts, *rights, *tables),
            [SMEM] + [VMEM] * (2 * len(segments) + len(tables)),
            (shape((rows, wide)),),
            (VMEM,),
            8 + volume // MIB,
            "outer_" + name + str(which),
            scratch=[pltpu.VMEM((half * size, left.shape[1]), LOW) for left in lefts] if direct else [],
        )[0]

    def fly(self, name, values):
        step = self.steps.get(name, 0)
        bits = bits_of(PIECES[name][0], self.count)
        self.flying[name] = swap(values, DP, self.count, bits[step])
        self.steps[name] = step + 1

    def send(self, name):
        self.fly(name, self.outer(name, 0))

    def keep(self, name):
        self.held[name] = self.outer(name, 1)

    def fold(self, name):
        if name in self.done:
            return
        keep, recv = self.held[name], self.flying[name]
        more = EXTRA if name in self.extra else 0
        rows = keep.shape[0] - more
        wide = keep.shape[1]
        if self.steps[name] == self.count.bit_length() - 1:
            (self.done[name],) = self.chain(
                add_body,
                (keep, recv),
                [VMEM, VMEM],
                (shape(keep.shape),),
                (VMEM,),
                4 + (keep.size * 12) // MIB,
                "last_" + name,
            )
        elif rows % 32:
            total = keep + recv
            tables = total[rows:]
            self.held[name] = jnp.concatenate([total[rows // 2 : rows], tables])
            self.fly(name, jnp.concatenate([total[: rows // 2], tables]))
        else:
            first, self.held[name] = self.chain(
                fold_extra_body if more else fold_body,
                (keep, recv),
                [VMEM, VMEM],
                (shape((rows // 2 + more, wide)),) * 2,
                (VMEM, VMEM),
                4 + (keep.size * 14) // MIB,
                "fold_" + name + str(self.steps[name]),
            )
            self.fly(name, first)

    def finish(self):
        while len(self.done) < len(PIECES):
            for name in PIECES:
                self.fold(name)


PLAN = (
    "ffn", "S:b", "S:a", "cross", "K:c", "K:b", "S:c", "self", "turnx", "K:a", "K:e", "S:e", "F:a",
    "F:b", "S:d", "in", "F:c", "F:e", "F:a", "K:d", "F:b", "F:d", "F:c", "store", "F:e", "F:a", "F:b",
    "F:c", "rest", "F:e", "F:d", "F:b", "F:c", "F:d", "F:a", "F:e", "F:d",
)


def per_device(
    count,
    inputs,
    datastore,
    lengths,
    indices,
    w_query,
    b_query,
    w_key,
    w_value,
    b_value,
    w_out,
    b_out,
    g_one,
    c_one,
    wc_query,
    bc_query,
    wc_key,
    wc_value,
    bc_value,
    wc_out,
    bc_out,
    g_two,
    c_two,
    w_up,
    b_up,
    w_down,
    b_down,
    g_three,
    c_three,
    cotangent,
):
    x = inputs[0]
    memory = datastore[0]
    q_scale = 1.0 / math.sqrt(HD)
    rank = lax.axis_index(DP).astype(jnp.int32)
    own = rank.reshape(1)
    side = lax.axis_index(TENSOR).astype(jnp.int32).reshape(1)
    chain = Chain()
    sources = {}
    sums = Sums(chain, own, count, sources)

    def other_core(values):
        return lax.ppermute(values, TENSOR, [(0, 1), (1, 0)])

    q, k, v, probs, inverse, ot, attended, self_part = self_forward(
        chain, lengths, x, w_query, b_query, w_key, w_value, b_value, w_out
    )
    self_other = other_core(self_part)
    words = mask_words(chain, indices[0])
    keys, values_t = store_products(chain, memory, wc_key, wc_value, True)
    unit_one, inv_one, one_t, cross_query, cross_probs, cross_sums, cross_ot, context, cross_part = cross_forward(
        chain, x, self_part, self_other, b_out, g_one, c_one, wc_query, bc_query, words, keys, values_t, bc_value, wc_out
    )
    cross_other = other_core(cross_part)
    values, keys_t = store_products(chain, memory, wc_key, wc_value, False)
    unit_two, inv_two, two_t, hidden, slope, ffn_part = ffn_forward(
        chain, unit_one, g_one, c_one, cross_part, cross_other, bc_out, g_two, c_two, w_up, b_up, w_down
    )
    ffn_other = other_core(ffn_part)
    memory_t = turn(chain, memory)
    output, grad_three, grad_ffn, ffn_t, sums_three = norm_three(
        chain, unit_two, g_two, c_two, ffn_part, ffn_other, b_down, g_three, c_three, cotangent[0]
    )
    sources["down"] = (ffn_t, hidden)
    half = memory.shape[0] // 2
    rows, wide = x.shape
    cols = w_query.shape[1]
    g = Bag()

    def do_ffn():
        g.pre, g.sums_up, g.two_part = ffn_backward(chain, grad_ffn, w_down, slope, w_up)
        g.two_other = other_core(g.two_part)
        sources["up"] = (two_t, g.pre)

    def do_cross():
        g.two, cross_t, g.sums_two, g.sums_cross, g.keys, g.values, asked, g.one_part = cross_backward(
            chain, grad_three, g.two_part, g.two_other, unit_two, inv_two, g_two, wc_out, cross_ot, cross_sums,
            cross_probs, values, keys_t, cross_query, wc_query,
        )
        g.one_other = other_core(g.one_part)
        sources["key"] = (memory_t, g.keys)
        sources["value"] = (memory_t, g.values)
        sources["mix"] = (cross_t, context)
        sources["ask"] = (one_t, asked)

    def do_self():
        g.one, self_t, sums_one, sums_self, grad_q, grad_k, grad_v, g.in_part = self_backward(
            chain, g.two, g.one_part, g.one_other, unit_one, inv_one, g_one, w_out, ot, inverse, probs,
            q, k, v, w_query, w_key, w_value,
        )
        g.in_other = other_core(g.in_part)
        g.q, g.k, g.v = grad_q, grad_k, grad_v
        sources["out"] = (self_t, attended)
        sums.extra[EXTRA_PIECE] = [sums_three, g.sums_two, sums_one, sums_self, g.sums_cross, g.sums_up]

    def do_turn_x():
        x_t = turn(chain, x)
        sources["q"] = (x_t, g.q)
        sources["k"] = (x_t, g.k)
        sources["v"] = (x_t, g.v)

    def do_in():
        block = pl.BlockSpec((rows // 4, wide), lambda i: (i, 0))
        (g.input,) = chain(
            add_two_body,
            (g.one, g.in_part, g.in_other),
            [block] * 3,
            (shape((rows, wide)),),
            (block,),
            12,
            "input_sum",
            grid=4,
        )

    def do_store():
        (part,) = chain(
            functools.partial(store_term_body, flipped=True),
            (side, g.keys, g.values, wc_key, wc_value),
            [SMEM] + [VMEM] * 4,
            (shape((half, wide)),),
            (VMEM,),
            20,
            "store_other",
        )
        g.store_other = other_core(part)

    def do_rest():
        (g.store,) = chain(
            store_sum_body,
            (side, g.keys, g.values, wc_key, wc_value, g.store_other),
            [SMEM] + [VMEM] * 5,
            (shape((half, wide)),),
            (VMEM,),
            24,
            "store_own",
        )

    jobs = {"turnx": do_turn_x, "ffn": do_ffn, "cross": do_cross, "self": do_self, "in": do_in, "store": do_store, "rest": do_rest}
    verbs = {"S": sums.send, "K": sums.keep, "F": sums.fold}
    for step in PLAN:
        verb, _, name = step.partition(":")
        if name:
            verbs[verb](name)
        else:
            jobs[verb]()
    sums.finish()
    input_grad = g.input[None]
    datastore_grad = g.store

    found = {}
    for name, (_, segments) in PIECES.items():
        start = 0
        for source, first, last in segments:
            span = (last - first) * UNIT
            found.setdefault(source, []).append(sums.done[name][: wide // count, start : start + span])
            start += span
    found = {source: jnp.concatenate(blocks, axis=1) for source, blocks in found.items()}
    table = sums.done[EXTRA_PIECE][wide // count :, :wide]
    mine = lax.dynamic_slice_in_dim(table[:9], rank * (wide // count), wide // count, axis=1)
    pairs = table[9:11].reshape(4, cols)
    pairs = lax.dynamic_slice_in_dim(pairs, rank * (cols // count), cols // count, axis=1)
    ups = table[11 : 11 + w_up.shape[1] // wide].reshape(-1)
    grad_b_up = lax.dynamic_slice_in_dim(ups, rank * (ups.shape[0] // count), ups.shape[0] // count)
    return (
        output[None],
        input_grad,
        datastore_grad[None],
        found["q"] * q_scale,
        pairs[0],
        found["k"],
        found["v"],
        pairs[1],
        found["out"].T,
        mine[8],
        mine[6],
        mine[7],
        found["ask"] * q_scale,
        pairs[3],
        found["key"],
        found["value"],
        pairs[2],
        found["mix"].T,
        mine[5],
        mine[3],
        mine[4],
        found["up"],
        grad_b_up,
        found["down"].T,
        mine[2],
        mine[0],
        mine[1],
    )


def solution(mesh):
    return jax.shard_map(
        functools.partial(per_device, mesh.shape[DP]),
        mesh=mesh,
        in_specs=(
            P(DP, None, None),
            P(DP, None, None),
            P(DP),
            P(DP, None, None),
            P(None, TENSOR),
            P(TENSOR),
            P(None, TENSOR),
            P(None, TENSOR),
            P(TENSOR),
            P(TENSOR, None),
            P(),
            P(),
            P(),
            P(None, TENSOR),
            P(TENSOR),
            P(None, TENSOR),
            P(None, TENSOR),
            P(TENSOR),
            P(TENSOR, None),
            P(),
            P(),
            P(),
            P(None, TENSOR),
            P(TENSOR),
            P(TENSOR, None),
            P(),
            P(),
            P(),
            P(DP, None, None),
        ),
        out_specs=(
            P(DP, None, None),
            P(DP, None, None),
            P(DP, TENSOR, None),
            P(DP, TENSOR),
            P((TENSOR, DP)),
            P(DP, TENSOR),
            P(DP, TENSOR),
            P((TENSOR, DP)),
            P(TENSOR, DP),
            P(DP),
            P(DP),
            P(DP),
            P(DP, TENSOR),
            P((TENSOR, DP)),
            P(DP, TENSOR),
            P(DP, TENSOR),
            P((TENSOR, DP)),
            P(TENSOR, DP),
            P(DP),
            P(DP),
            P(DP),
            P(DP, TENSOR),
            P((TENSOR, DP)),
            P(TENSOR, DP),
            P(DP),
            P(DP),
            P(DP),
        ),
        check_vma=False,
    )
```

```python
import functools
import math

import jax
import jax.numpy as jnp
from jax import lax
from jax.experimental import pallas as pl
from jax.experimental.pallas import tpu as pltpu
from jax.sharding import PartitionSpec as P

HD = 64
NEG = -1e30
EPS = 1e-05
WORDS = 256
MIB = 1 << 20

F32 = jnp.float32
DP = "dp"
TENSOR = "tensor"
LOW = jnp.bfloat16


def nn(left, right):
    return lax.dot_general(left, right, (((1,), (0,)), ((), ())), preferred_element_type=F32)


def nt(left, right):
    return lax.dot_general(left, right, (((1,), (1,)), ((), ())), preferred_element_type=F32)


def tn(left, right):
    return lax.dot_general(left, right, (((0,), (0,)), ((), ())), preferred_element_type=F32)


def flip(values):
    return values.astype(F32).T


def row(ref):
    return ref[...].astype(F32).reshape(1, -1)


def spread_row(ref, out):
    values = row(ref)
    wide = out.shape[1]
    for i in range(out.shape[0]):
        out[i : i + 1, :] = values[:, i * wide : (i + 1) * wide]


def shape(dims, kind=F32):
    return jax.ShapeDtypeStruct(dims, kind)


VMEM = pl.BlockSpec(memory_space=pltpu.VMEM)
SMEM = pl.BlockSpec(memory_space=pltpu.SMEM)
ANY = pl.BlockSpec(memory_space=pl.ANY)


def whole(dims):
    return pl.BlockSpec(dims, lambda i: (0,) * len(dims), pipeline_mode=pl.Buffered(1))


def kept(dims):
    return pl.BlockSpec(dims, lambda i: (0,) * len(dims))


WEIGHTS = {"cross_b": 10000000000, "self_b": 1000000000, "fold_c": 1, "fold_b": 6000000000, "fold_d": 20000000000, "ffn_b": 6000000000, "outer": 10000000000, "fold": 40000000000, "": 1}


def weight_of(name):
    return next(weight for prefix, weight in WEIGHTS.items() if name.startswith(prefix))


class Chain:
    def __init__(self):
        self.token = None

    def __call__(self, body, args, ins, shapes, outs, mib, name, grid=None, scratch=()):
        given = len(args)
        extra = [] if self.token is None else [pltpu.with_memory_space_constraint(self.token, pltpu.HBM)]

        def kernel(*refs):
            refs = list(refs)
            token = refs.pop(given + len(extra) + len(shapes))
            del refs[given : given + len(extra)]
            body(*refs)
            token[...] = jnp.zeros_like(token)

        more = {} if grid is None else {"grid": (grid,)}
        args = [
            pltpu.with_memory_space_constraint(arg, pltpu.HBM) if spec.memory_space in (None, pl.ANY) else arg
            for arg, spec in zip(args, ins)
        ]
        shapes = [
            pltpu.HBM(out.shape, out.dtype) if spec.memory_space is None else out for out, spec in zip(shapes, outs)
        ]
        results = pl.pallas_call(
            kernel,
            out_shape=(*shapes, pltpu.HBM((8, 128), F32)),
            in_specs=[*ins, *([ANY] * len(extra))],
            out_specs=(*outs, whole((8, 128)) if grid else pl.BlockSpec((8, 128))),
            scratch_shapes=list(scratch),
            compiler_params=pltpu.CompilerParams(vmem_limit_bytes=mib * MIB),
            cost_estimate=pl.CostEstimate(flops=weight_of(name), bytes_accessed=1, transcendentals=0),
            name=name,
            **more,
        )(*args, *extra)
        self.token = results[-1]
        return results[:-1]


def norm_parts(values):
    average = jnp.mean(values, axis=-1, keepdims=True)
    centred = values - average
    variance = jnp.mean(centred * centred, axis=-1, keepdims=True)
    inverse = lax.rsqrt(variance + EPS)
    return centred * inverse, inverse


def norm_back(grad, gain, unit, inverse):
    scaled = grad * gain
    first = jnp.mean(scaled, axis=-1, keepdims=True)
    second = jnp.mean(scaled * unit, axis=-1, keepdims=True)
    return inverse * (scaled - first - unit * second)


def rows_of_half(values, half):
    place = lax.broadcasted_iota(jnp.int32, values.shape, 0)
    return jnp.where((place // HD) == half, values, jnp.zeros_like(values))


def lanes_of_half(values, half):
    place = lax.broadcasted_iota(jnp.int32, values.shape, 1)
    return jnp.where((place // HD) == half, values, jnp.zeros_like(values))


def self_forward_body(
    length, x, wq, bq, wk, wv, bv, wo,
    q_out, k_out, v_out, p_out, inv_out, ot_out, att_out, part_out,
    bias, q_low, k_low, v_low, probs, done,
):
    rows = x.shape[0]
    heads = wq.shape[1] // HD
    q_scale = 1.0 / math.sqrt(HD)
    copies = []

    def leave(source, target):
        copy = pltpu.make_async_copy(source, target, done.at[len(copies)])
        copy.start()
        copies.append(copy)

    x_low = x[...]
    q = ((nn(x_low, wq[...]) + row(bq)) * q_scale).astype(LOW)
    k = nn(x_low, wk[...]).astype(LOW)
    v = (nn(x_low, wv[...]) + row(bv)).astype(LOW)
    q_low[...] = q
    k_low[...] = k
    v_low[...] = v
    leave(q_low, q_out)
    leave(k_low, k_out)
    leave(v_low, v_out)
    qt = flip(q).astype(LOW)
    vt = flip(v).astype(LOW)
    key = lax.broadcasted_iota(jnp.int32, (rows, rows), 0)
    query = lax.broadcasted_iota(jnp.int32, (rows, rows), 1)
    bias[...] = jnp.where((key <= query) & (key < length[0]), 0.0, NEG)
    for head in range(heads):
        pair, half = head // 2, head % 2
        lanes = slice(pair * 2 * HD, (pair + 1) * 2 * HD)
        own = slice(head * HD, (head + 1) * HD)
        scores = nn(k[:, lanes], rows_of_half(qt[lanes], half)) + bias[...]
        top = jnp.max(scores, axis=0, keepdims=True)
        grown = jnp.exp(scores - top)
        inverse = 1.0 / jnp.sum(grown, axis=0, keepdims=True)
        low = grown.astype(LOW)
        probs[head] = low
        leave(probs.at[head], p_out.at[head])
        inv_out[pair, half : half + 1, :] = inverse
        ot_out[own, :] = nn(vt[own], low) * inverse
    attended = ot_out[...].T.astype(LOW)
    att_out[...] = attended
    part_out[...] = nn(attended, wo[...])
    for copy in copies:
        copy.wait()


def self_forward(chain, length, x, wq, bq, wk, wv, bv, wo):
    rows, width = x.shape
    cols = wq.shape[1]
    heads = cols // HD
    pairs = heads // 2
    side = whole((width, cols))
    return chain(
        self_forward_body,
        (length, x, wq, bq, wk, wv, bv, wo),
        [SMEM, whole((rows, width)), side, whole((cols,)), side, side, whole((cols,)), whole((cols, width))],
        (
            pltpu.HBM((rows, cols), LOW),
            pltpu.HBM((rows, cols), LOW),
            pltpu.HBM((rows, cols), LOW),
            pltpu.HBM((heads, rows, rows), LOW),
            shape((pairs, 2, rows)),
            shape((cols, rows)),
            shape((rows, cols), LOW),
            shape((rows, width)),
        ),
        (
            ANY, ANY, ANY, ANY,
            whole((pairs, 2, rows)),
            whole((cols, rows)),
            whole((rows, cols)),
            VMEM,
        ),
        28,
        "self_forward",
        grid=1,
        scratch=[
            pltpu.VMEM((rows, rows), F32),
            pltpu.VMEM((rows, cols), LOW),
            pltpu.VMEM((rows, cols), LOW),
            pltpu.VMEM((rows, cols), LOW),
            pltpu.VMEM((heads, rows, rows), LOW),
            pltpu.SemaphoreType.DMA((heads + 3,)),
        ],
    )


def mask_body(picks, words, sums):
    step = pl.program_id(0)
    block = picks.shape[0]
    up = lax.broadcasted_iota(jnp.int32, (256, 256), 0)
    across = lax.broadcasted_iota(jnp.int32, (256, 256), 1)
    same = (up & 15) == (across & 15)
    for part in range(block // 16):
        index = picks[part * 16 : (part + 1) * 16, :]
        bit = lax.shift_left(jnp.ones_like(index), index >> 8).astype(F32).astype(LOW)
        upper = ((index >> 4) & 15).astype(F32).astype(LOW)
        lower = (index & 15).astype(F32).astype(LOW)
        zero = jnp.zeros_like(bit)
        one = jnp.ones_like(bit)
        left = jnp.concatenate([jnp.where(upper == c, bit, zero) for c in range(16)], axis=0)
        right = jnp.concatenate([jnp.where(lower == c, one, zero) for c in range(16)], axis=0)
        cross = jnp.where(same, nt(left, right), 0.0).astype(LOW)
        start = pl.multiple_of(step * block + part * 16, 16)
        for c in range(16):
            sums[pl.ds(start, 16), c * 256 : (c + 1) * 256] = cross[c * 16 : (c + 1) * 16, :]

    @pl.when(step == pl.num_programs(0) - 1)
    def _():
        word = lax.broadcasted_iota(jnp.int32, (256, 4096), 0)
        place = lax.broadcasted_iota(jnp.int32, (256, 4096), 1)
        fold = jnp.where((place >> 4) == word, 1.0, 0.0).astype(LOW)
        words[...] = nt(fold, sums[...]).astype(jnp.int32)


def mask_words(chain, picks):
    rows, chosen = picks.shape
    block = math.gcd(rows, 256)
    return chain(
        mask_body,
        (picks,),
        [pl.BlockSpec((block, chosen), lambda i: (i, 0))],
        (shape((WORDS, rows), jnp.int32),),
        (whole((WORDS, rows)),),
        28,
        "mask_words",
        grid=rows // block,
        scratch=[pltpu.VMEM((rows, 16 * 256), LOW)],
    )[0]


def put_pairs(out, values):
    high = values.astype(LOW)
    rest = (values - high.astype(F32)).astype(LOW)
    pair = 2 * HD
    for i in range(values.shape[1] // pair):
        out[:, 2 * i * pair : (2 * i + 1) * pair] = high[:, i * pair : (i + 1) * pair]
        out[:, (2 * i + 1) * pair : (2 * i + 2) * pair] = rest[:, i * pair : (i + 1) * pair]


def put_heads(out, values):
    high = values.astype(LOW)
    rest = (values - high.astype(F32)).astype(LOW)
    for i in range(values.shape[0] // HD):
        out[2 * i * HD : (2 * i + 1) * HD, :] = high[i * HD : (i + 1) * HD, :]
        out[(2 * i + 1) * HD : (2 * i + 2) * HD, :] = rest[i * HD : (i + 1) * HD, :]


def store_body(memory, wk, wv, k_out, vt_out):
    low = memory[...]
    put_pairs(k_out, nn(low, wk[...]))
    turned = (((0,), (1,)), ((), ()))
    put_heads(vt_out, lax.dot_general(wv[...], low, turned, preferred_element_type=F32))


def store_turned_body(memory, wk, wv, v_out, kt_out):
    low = memory[...]
    put_pairs(v_out, nn(low, wv[...]))
    turned = (((0,), (1,)), ((), ()))
    put_heads(kt_out, lax.dot_general(wk[...], low, turned, preferred_element_type=F32))


def store_products(chain, memory, wk, wv, first):
    entries, width = memory.shape
    cols = wk.shape[1]
    block = 1024
    return chain(
        store_body if first else store_turned_body,
        (memory, wk, wv),
        [pl.BlockSpec((block, width), lambda i: (i, 0)), whole((width, cols)), whole((width, cols))],
        (shape((entries, 2 * cols), LOW), shape((2 * cols, entries), LOW)),
        (pl.BlockSpec((block, 2 * cols), lambda i: (i, 0)), pl.BlockSpec((2 * cols, block), lambda i: (0, i))),
        32,
        "store_products" if first else "store_turned",
        grid=entries // block,
    )


def cross_forward_body(
    x, own, other, b_out, g_one, c_one, wq, bq, words, keys, values_t, bv, wo,
    unit_out, inv_out, turn_out, q_out, p_out, sum_out, ot_out, ctx_out, part_out,
    qt, bias, scores, keys_held, values_held, probs, loads, leaves,
):
    q_scale = 1.0 / math.sqrt(HD)
    entries = keys.shape[0]
    heads = wq.shape[1] // HD
    chunk = 1024
    wide = 4 * HD

    def load(pair):
        lanes = pl.ds(pl.multiple_of(pair * wide, wide), wide)
        return (
            pltpu.make_async_copy(keys.at[:, lanes], keys_held.at[pair], loads.at[0, pair]),
            pltpu.make_async_copy(values_t.at[lanes, :], values_held.at[pair], loads.at[1, pair]),
        )

    def leave(pair, half):
        return pltpu.make_async_copy(probs.at[half], p_out.at[2 * pair + half], leaves.at[half])

    for pair in range(heads // 2):
        for copy in load(pair):
            copy.start()
    total = x[...].astype(F32) + (own[...] + other[...] + row(b_out))
    unit, inverse = norm_parts(total)
    unit_out[...] = unit
    inv_out[...] = inverse
    low = (unit * row(g_one) + row(c_one)).astype(LOW)
    turn_out[...] = flip(low).astype(LOW)
    q = ((nn(low, wq[...]) + row(bq)) * q_scale).astype(LOW)
    q_out[...] = q
    qt[...] = flip(q).astype(LOW)
    held = words[...]
    for part in range(entries // WORDS):
        bias[part * WORDS : (part + 1) * WORDS, :] = jnp.where(((held >> part) & 1) == 1, 0.0, NEG)

    def one_pair(pair, carry):
        for copy in load(pair):
            copy.wait()
        pair_rows = qt[pl.ds(pl.multiple_of(pair * 2 * HD, 2 * HD), 2 * HD), :]
        for half in range(2):
            query = rows_of_half(pair_rows, half)
            query = jnp.concatenate([query, query], axis=0)
            top = None
            for part in range(entries // chunk):
                span = slice(part * chunk, (part + 1) * chunk)
                piece = nn(keys_held[pair, span, :], query) + bias[span, :]
                scores[half, span, :] = piece
                peak = jnp.max(piece.reshape(chunk // 8, 8, -1), axis=0)
                top = peak if top is None else jnp.maximum(top, peak)
            top = jnp.max(top, axis=0, keepdims=True)

            @pl.when(pair > 0)
            def _():
                leave(pair - 1, half).wait()

            total = pooled = None
            for part in range(entries // chunk):
                span = slice(part * chunk, (part + 1) * chunk)
                grown = jnp.exp(scores[half, span, :] - top)
                low = grown.astype(LOW)
                probs[half, span, :] = low
                mass = jnp.sum(grown.reshape(chunk // 8, 8, -1), axis=0)
                term = nn(values_held[pair, half * 2 * HD : (half + 1) * 2 * HD, span], low)
                total, pooled = (mass, term) if total is None else (total + mass, pooled + term)
            leave(pair, half).start()
            inverse = 1.0 / jnp.sum(total, axis=0, keepdims=True)
            head = 2 * pair + half
            sum_out[pl.ds(head, 1), :] = inverse
            ot_out[pl.ds(pl.multiple_of(head * HD, HD), HD), :] = (pooled[:HD] + pooled[HD:]) * inverse
        return carry

    lax.fori_loop(0, heads // 2, one_pair, 0)
    context = (ot_out[...].T + row(bv)).astype(LOW)
    ctx_out[...] = context
    part_out[...] = nn(context, wo[...])
    for half in range(2):
        leave(heads // 2 - 1, half).wait()


def cross_forward(chain, x, own, other, b_out, g_one, c_one, wq, bq, words, keys, values_t, bv, wo):
    rows, width = x.shape
    entries = keys.shape[0]
    cols = wq.shape[1]
    heads = cols // HD
    line = whole((width,))
    thin = whole((cols,))
    return chain(
        cross_forward_body,
        (x, own, other, b_out, g_one, c_one, wq, bq, words, keys, values_t, bv, wo),
        [whole((rows, width)), VMEM, VMEM, line, line, line, whole((width, cols)), thin, whole((WORDS, rows)),
         ANY, ANY, thin, whole((cols, width))],
        (
            shape((rows, width)),
            shape((rows, 1)),
            shape((width, rows), LOW),
            shape((rows, cols), LOW),
            pltpu.HBM((heads, entries, rows), LOW),
            shape((heads, rows)),
            shape((cols, rows)),
            shape((rows, cols), LOW),
            shape((rows, width)),
        ),
        (VMEM, whole((rows, 1)), VMEM, VMEM, ANY, VMEM, whole((cols, rows)), VMEM, VMEM),
        38,
        "cross_forward",
        grid=1,
        scratch=[
            pltpu.VMEM((cols, rows), LOW),
            pltpu.VMEM((entries, rows), F32),
            pltpu.VMEM((2, entries, rows), F32),
            pltpu.VMEM((heads // 2, entries, 4 * HD), LOW),
            pltpu.VMEM((heads // 2, 4 * HD, entries), LOW),
            pltpu.VMEM((2, entries, rows), LOW),
            pltpu.SemaphoreType.DMA((2, heads // 2)),
            pltpu.SemaphoreType.DMA((2,)),
        ],
    )


def ffn_forward_body(
    unit_one, g_one, c_one, own, other, b_out, g_two, c_two, w_up, b_up, w_down,
    unit_out, inv_out, turn_out, hid_out, slope_out, part_out, low_two, bias,
):
    step = pl.program_id(0)

    @pl.when(step == 0)
    def _():
        total = unit_one[...] * row(g_one) + row(c_one) + (own[...] + other[...] + row(b_out))
        unit, inverse = norm_parts(total)
        unit_out[...] = unit
        inv_out[...] = inverse
        low = (unit * row(g_two) + row(c_two)).astype(LOW)
        low_two[...] = low
        spread_row(b_up, bias)
        turn_out[...] = flip(low).astype(LOW)

    pre = nn(low_two[...], w_up[...]) + bias[pl.ds(step, 1), :]
    below = 0.5 * (1.0 + lax.erf(pre * math.sqrt(0.5)))
    density = jnp.exp(-0.5 * pre * pre) * (1.0 / math.sqrt(2.0 * math.pi))
    lanes = pl.ds(pl.multiple_of(step * pre.shape[1], pre.shape[1]), pre.shape[1])
    slope_out[...] = below + pre * density
    hidden = (pre * below).astype(LOW)
    hid_out[:, lanes] = hidden
    term = nn(hidden, w_down[...])

    @pl.when(step == 0)
    def _():
        part_out[...] = term

    @pl.when(step > 0)
    def _():
        part_out[...] += term


def ffn_forward(chain, unit_one, g_one, c_one, own, other, b_out, g_two, c_two, w_up, b_up, w_down):
    rows, width = unit_one.shape
    units = w_up.shape[1]
    block = 768
    return chain(
        ffn_forward_body,
        (unit_one, g_one, c_one, own, other, b_out, g_two, c_two, w_up, b_up, w_down),
        [
            VMEM,
            whole((width,)),
            whole((width,)),
            VMEM,
            VMEM,
            whole((width,)),
            whole((width,)),
            whole((width,)),
            pl.BlockSpec((width, block), lambda i: (0, i)),
            whole((units,)),
            pl.BlockSpec((block, width), lambda i: (i, 0)),
        ],
        (
            shape((rows, width)),
            shape((rows, 1)),
            shape((width, rows), LOW),
            shape((rows, units), LOW),
            shape((rows, units)),
            shape((rows, width)),
        ),
        (VMEM, whole((rows, 1)), whole((width, rows)), VMEM, pl.BlockSpec((rows, block), lambda i: (0, i)), VMEM),
        30,
        "ffn_forward",
        grid=units // block,
        scratch=[pltpu.VMEM((rows, width), LOW), pltpu.VMEM((units // block, block), F32)],
    )


def norm_three_body(unit_two, g_two, c_two, own, other, b_down, g_three, c_three, cotangent, out, grad, low, turn, sums):
    step = pl.program_id(0)
    block = out.shape[0]
    span = pl.ds(pl.multiple_of(step * block, block), block)
    total = unit_two[span, :] * row(g_two) + row(c_two) + (own[span, :] + other[span, :] + row(b_down))
    unit, inverse = norm_parts(total)
    out[...] = (unit * row(g_three) + row(c_three)).astype(LOW)
    seed = cotangent[...].astype(F32)
    back = norm_back(seed, row(g_three), unit, inverse)
    rounded = back.astype(LOW)
    grad[span, :] = back
    low[span, :] = rounded
    turn[:, span] = flip(rounded).astype(LOW)

    @pl.when(step == 0)
    def _():
        sums[...] = jnp.zeros_like(sums)

    sums[0:1, :] += jnp.sum(seed * unit, axis=0, keepdims=True)
    sums[1:2, :] += jnp.sum(seed, axis=0, keepdims=True)
    sums[2:3, :] += jnp.sum(rounded.astype(F32), axis=0, keepdims=True)


def norm_three(chain, *args):
    rows, width = args[0].shape
    block = rows
    tall = pl.BlockSpec((block, width), lambda i: (i, 0))
    line = whole((width,))
    return chain(
        norm_three_body,
        args,
        [VMEM, line, line, VMEM, VMEM, line, line, line, tall],
        (
            shape((rows, width), LOW),
            shape((rows, width)),
            shape((rows, width), LOW),
            shape((width, rows), LOW),
            shape((3, width)),
        ),
        (tall, VMEM, VMEM, VMEM, VMEM),
        20,
        "norm_three",
        grid=1,
    )


def ffn_backward_body(grad, w_down, slope, w_up, pre_out, sum_out, part_out):
    step = pl.program_id(0)
    block = w_down.shape[0]
    lanes = pl.ds(pl.multiple_of(step * block, block), block)
    back = (nt(grad[...], w_down[...]) * slope[...]).astype(LOW)
    pre_out[:, lanes] = back
    sum_out[:, lanes] = jnp.sum(back.astype(F32), axis=0, keepdims=True)
    term = nt(back, w_up[...])

    @pl.when(step == 0)
    def _():
        part_out[...] = term

    @pl.when(step > 0)
    def _():
        part_out[...] += term


def ffn_backward(chain, grad, w_down, slope, w_up):
    rows, width = grad.shape
    units = w_up.shape[1]
    block = 768
    return chain(
        ffn_backward_body,
        (grad, w_down, slope, w_up),
        [
            VMEM,
            pl.BlockSpec((block, width), lambda i: (i, 0)),
            pl.BlockSpec((rows, block), lambda i: (0, i)),
            pl.BlockSpec((width, block), lambda i: (0, i)),
        ],
        (shape((rows, units), LOW), shape((1, units)), shape((rows, width))),
        (VMEM, whole((1, units)), VMEM),
        26,
        "ffn_backward",
        grid=units // block,
    )


def cross_backward_body(
    grad_three, own, other, unit_two, inv_two, g_two, wo, ot, sums, probs, values, keys_t, query, wq,
    grad_out, turn_out, norm_sums, head_sums, dk_out, dv_out, dq_out, part_out,
    dctx_t, dq_t, change, grad_held, probs_held, values_held, keys_held, loads, brings, done,
):
    q_scale = 1.0 / math.sqrt(HD)
    entries = values.shape[0]
    cols = wq.shape[1]
    heads = cols // HD
    chunk = 1024
    wide = 4 * HD

    def load(pair):
        lanes = pl.ds(pl.multiple_of(pair * wide, wide), wide)
        return (
            pltpu.make_async_copy(values.at[:, lanes], values_held.at[pair], loads.at[0, pair]),
            pltpu.make_async_copy(keys_t.at[lanes, :], keys_held.at[pair], loads.at[1, pair]),
        )

    def bring(pair, half):
        return pltpu.make_async_copy(probs.at[2 * pair + half], probs_held.at[half], brings.at[half])

    bring(0, 0).start()
    for pair in range(heads // 2):
        for copy in load(pair):
            copy.start()
        if pair == 0:
            bring(0, 1).start()
    grad_in = grad_three[...] + (own[...] + other[...])
    unit = unit_two[...]
    grad = norm_back(grad_in, row(g_two), unit, inv_two[...])
    grad_held[...] = grad
    keep = pltpu.make_async_copy(grad_held, grad_out, done)
    keep.start()
    low = grad.astype(LOW)
    turn_out[...] = flip(low).astype(LOW)
    norm_sums[0:1, :] = jnp.sum(grad_in * unit, axis=0, keepdims=True)
    norm_sums[1:2, :] = jnp.sum(grad_in, axis=0, keepdims=True)
    norm_sums[2:3, :] = jnp.sum(low.astype(F32), axis=0, keepdims=True)
    dctx_t[...] = nt(wo[...], low)
    head_sums[0:1, :cols] = jnp.sum(dctx_t[...].T, axis=0, keepdims=True)

    def one_pair(pair, carry):
        for copy in load(pair):
            copy.wait()
        lanes = pl.ds(pl.multiple_of(pair * 2 * HD, 2 * HD), 2 * HD)
        pair_query = query[:, lanes]
        for half in range(2):
            head = 2 * pair + half
            own_rows = pl.ds(pl.multiple_of(head * HD, HD), HD)
            scaled = (dctx_t[own_rows, :] * sums[pl.ds(head, 1), :]).astype(LOW)
            inner = jnp.sum(scaled.astype(F32) * ot[own_rows, :], axis=0, keepdims=True)
            empty = jnp.zeros_like(scaled)
            grad_rows = jnp.concatenate([scaled, empty] if half == 0 else [empty, scaled], axis=0)
            own_grad = flip(grad_rows).astype(LOW)
            grad_rows = jnp.concatenate([grad_rows, grad_rows], axis=0)
            own_query = lanes_of_half(pair_query, half)
            bring(pair, half).wait()
            for part in range(entries // chunk):
                span = slice(part * chunk, (part + 1) * chunk)
                low_probs = probs_held[half, span, :]
                shift = nn(values_held[pair, span, :], grad_rows) - inner
                delta = (low_probs.astype(F32) * shift).astype(LOW)
                change[half, span, :] = delta
                k_term = nn(delta, own_query).astype(LOW)
                v_term = nn(low_probs, own_grad).astype(LOW)
                if half == 0:
                    dk_out[span, lanes] = k_term
                    dv_out[span, lanes] = v_term
                else:
                    dk_out[span, lanes] = dk_out[span, lanes] + k_term
                    dv_out[span, lanes] = dv_out[span, lanes] + v_term

            @pl.when(pair + 1 < heads // 2)
            def _():
                bring(pair + 1, half).start()

            both = nn(keys_held[pair, half * 2 * HD : (half + 1) * 2 * HD, :], change[half])
            dq_t[own_rows, :] = both[:HD] + both[HD:]
        return carry

    lax.fori_loop(0, heads // 2, one_pair, 0)
    dq = dq_t[...].T.astype(LOW)
    dq_out[...] = dq
    head_sums[0:1, cols:] = jnp.sum(dq.astype(F32), axis=0, keepdims=True) * q_scale
    part_out[...] = nt(dq, wq[...]) * q_scale
    keep.wait()


def cross_backward(chain, *args):
    rows, width = args[0].shape
    entries = args[10].shape[0]
    cols = args[13].shape[1]
    heads = cols // HD
    return chain(
        cross_backward_body,
        args,
        [VMEM, VMEM, VMEM, VMEM, whole((rows, 1)), whole((width,)), whole((cols, width)), whole((cols, rows)), VMEM,
         ANY, ANY, ANY, VMEM, whole((width, cols))],
        (
            pltpu.HBM((rows, width), F32),
            shape((width, rows), LOW),
            shape((3, width)),
            shape((1, 2 * cols)),
            shape((entries, cols), LOW),
            shape((entries, cols), LOW),
            shape((rows, cols), LOW),
            shape((rows, width)),
        ),
        (ANY, VMEM, whole((3, width)), whole((1, 2 * cols)), VMEM, VMEM, VMEM, VMEM),
        32,
        "cross_backward",
        grid=1,
        scratch=[
            pltpu.VMEM((cols, rows), F32),
            pltpu.VMEM((cols, rows), F32),
            pltpu.VMEM((2, entries, rows), LOW),
            pltpu.VMEM((rows, width), F32),
            pltpu.VMEM((2, entries, rows), LOW),
            pltpu.VMEM((heads // 2, entries, 4 * HD), LOW),
            pltpu.VMEM((heads // 2, 4 * HD, entries), LOW),
            pltpu.SemaphoreType.DMA((2, heads // 2)),
            pltpu.SemaphoreType.DMA((2,)),
            pltpu.SemaphoreType.DMA,
        ],
    )


def self_backward_body(
    grad_two, own, other, unit_one, inv_one, g_one, wo, ot, inverse, probs, q, k, v, wq, wk, wv,
    grad_out, turn_out, norm_sums, head_sums, dq_out, dk_out, dv_out, part_out,
    datt_t, grad_held, done,
):
    step = pl.program_id(0)
    q_scale = 1.0 / math.sqrt(HD)
    cols = datt_t.shape[0]

    @pl.when(step == 0)
    def _():
        grad_in = grad_two[...] + (own[...] + other[...])
        unit = unit_one[...]
        grad = norm_back(grad_in, row(g_one), unit, inv_one[...])
        grad_held[...] = grad
        pltpu.make_async_copy(grad_held, grad_out, done).start()
        low = grad.astype(LOW)
        turn_out[...] = flip(low).astype(LOW)
        norm_sums[0:1, :] = jnp.sum(grad_in * unit, axis=0, keepdims=True)
        norm_sums[1:2, :] = jnp.sum(grad_in, axis=0, keepdims=True)
        norm_sums[2:3, :] = jnp.sum(low.astype(F32), axis=0, keepdims=True)
        datt_t[...] = nt(wo[...], low)

    pair_grad = datt_t[pl.ds(pl.multiple_of(step * 2 * HD, 2 * HD), 2 * HD), :]
    place = lax.broadcasted_iota(jnp.int32, pair_grad.shape, 0)
    scaled = pair_grad * jnp.where(place < HD, inverse[0, 0:1, :], inverse[0, 1:2, :])
    scaled_low = scaled.astype(LOW)
    weighed = scaled_low.astype(F32) * ot[...]
    scaled_rows = flip(scaled_low).astype(LOW)
    pair_query = q[...]
    pair_values = v[...]
    keys_t = flip(k[...]).astype(LOW)
    dk = None
    dv = None
    dq_t = []
    for half in range(2):
        inner = jnp.sum(weighed[half * HD : (half + 1) * HD, :], axis=0, keepdims=True)
        low_probs = probs[half]
        shift = nn(pair_values, rows_of_half(scaled_low, half)) - inner
        delta = (low_probs.astype(F32) * shift).astype(LOW)
        k_term = nn(delta, lanes_of_half(pair_query, half))
        v_term = nn(low_probs, lanes_of_half(scaled_rows, half))
        dk = k_term if dk is None else dk + k_term
        dv = v_term if dv is None else dv + v_term
        dq_t.append(nn(keys_t[half * HD : (half + 1) * HD], delta))
    dq = jnp.concatenate(dq_t, axis=0).T.astype(LOW)
    dk_low = dk.astype(LOW)
    dv_low = dv.astype(LOW)
    lanes = pl.ds(pl.multiple_of(step * 2 * HD, 2 * HD), 2 * HD)
    dq_out[:, lanes] = dq
    dk_out[:, lanes] = dk_low
    dv_out[:, lanes] = dv_low
    later = pl.ds(pl.multiple_of(cols + step * 2 * HD, 2 * HD), 2 * HD)
    head_sums[0:1, lanes] = jnp.sum(dq.astype(F32), axis=0, keepdims=True) * q_scale
    head_sums[0:1, later] = jnp.sum(dv_low.astype(F32), axis=0, keepdims=True)
    term = nt(dq, wq[...]) * q_scale + nt(
        jnp.concatenate([dk_low, dv_low], axis=1), jnp.concatenate([wk[...], wv[...]], axis=1)
    )

    @pl.when(step == 0)
    def _():
        part_out[...] = term

    @pl.when(step > 0)
    def _():
        part_out[...] += term

    @pl.when(step == pl.num_programs(0) - 1)
    def _():
        pltpu.make_async_copy(grad_held, grad_out, done).wait()


def self_backward(chain, *args):
    rows, width = args[0].shape
    cols = args[10].shape[1]
    pairs = cols // (2 * HD)
    tall = pl.BlockSpec((rows, 2 * HD), lambda i: (0, i))
    side = pl.BlockSpec((width, 2 * HD), lambda i: (0, i))
    return chain(
        self_backward_body,
        args,
        [
            whole((rows, width)),
            VMEM,
            VMEM,
            whole((rows, width)),
            whole((rows, 1)),
            whole((width,)),
            whole((cols, width)),
            pl.BlockSpec((2 * HD, rows), lambda i: (i, 0)),
            pl.BlockSpec((1, 2, rows), lambda i: (i, 0, 0)),
            pl.BlockSpec((2, rows, rows), lambda i: (i, 0, 0)),
            tall, tall, tall, side, side, side,
        ],
        (
            pltpu.HBM((rows, width), F32),
            shape((width, rows), LOW),
            shape((3, width)),
            shape((1, 2 * cols)),
            shape((rows, cols), LOW),
            shape((rows, cols), LOW),
            shape((rows, cols), LOW),
            shape((rows, width)),
        ),
        (ANY, VMEM, whole((3, width)), whole((1, 2 * cols)), VMEM, VMEM, VMEM, VMEM),
        18,
        "self_backward",
        grid=pairs,
        scratch=[pltpu.VMEM((cols, rows), F32), pltpu.VMEM((rows, width), F32), pltpu.SemaphoreType.DMA],
    )


def store_term_body(side, keys, values, wk, wv, out, *, flipped):
    rows = out.shape[0]
    which = 1 - side[0] if flipped else side[0]
    span = pl.ds(pl.multiple_of(which * rows, rows), rows)
    out[...] = nt(keys[span, :], wk[...]) + nt(values[span, :], wv[...])


def store_sum_body(side, keys, values, wk, wv, other, out):
    store_term_body(side, keys, values, wk, wv, out, flipped=False)
    out[...] += other[...]


def turn_body(values, out):
    out[...] = flip(values[...]).astype(LOW)


def turn(chain, values):
    rows, width = values.shape
    block = min(rows, 1024)
    return chain(
        turn_body,
        (values,),
        [pl.BlockSpec((block, width), lambda i: (i, 0))],
        (shape((width, rows), LOW),),
        (pl.BlockSpec((width, block), lambda i: (0, i)),),
        28,
        "turn",
        grid=rows // block,
    )[0]


BITS = {"x": 0, "y": 1, "l": 2, "h": 3}

PIECES = {
    "a": ("lhxy", (("down", 0, 11),)),
    "b": ("xlyh", (("down", 11, 12), ("up", 0, 12))),
    "c": ("yxlh", (("key", 0, 3), ("value", 0, 3), ("mix", 0, 3), ("ask", 0, 3))),
    "d": ("yxlh", (("q", 0, 3), ("k", 0, 3))),
    "e": ("xlyh", (("v", 0, 3), ("out", 0, 3))),
}
EXTRA_PIECE = "d"
UNIT = 128


def bits_of(letters, count):
    total = count.bit_length() - 1
    chosen = [BITS[letter] for letter in letters if BITS[letter] < total]
    return chosen + [bit for bit in range(total) if bit not in chosen]


def block_order(bits):
    count = len(bits)
    return [
        sum((1 - ((place >> (count - 1 - i)) & 1)) << bit for i, bit in enumerate(bits))
        for place in range(1 << count)
    ]


def swap(values, axis, count, bit):
    return lax.ppermute(values, axis, [(i, i ^ (1 << bit)) for i in range(count)])


def outer_body(*refs, parts, offsets, size, direct, tables):
    own, refs = refs[0], refs[1:]
    lefts, rights, refs = refs[:parts[0]], refs[parts[0] : 2 * parts[0]], refs[2 * parts[0] :]
    held, out, scratch = refs[:tables], refs[tables], refs[tables + 1 :]
    start = 0
    rows = len(offsets) * size
    for number, (first, last) in enumerate(parts[1:]):
        left = lefts[number]
        if direct:
            picked = scratch[number]
            for place, offset in enumerate(offsets):
                source = pl.multiple_of((own[0] ^ offset) * size, 16)
                picked[place * size : (place + 1) * size, :] = left[pl.ds(source, size), :]
            left = picked
        wide = (last - first) * UNIT
        out[:rows, start : start + wide] = nn(left[...], rights[number][:, first * UNIT : last * UNIT])
        start += wide
    if tables:
        out[rows:, :] = jnp.zeros((out.shape[0] - rows, out.shape[1]), F32)
        place = rows
        line = held[0].shape[1]
        for table in held:
            for i in range(table.shape[0]):
                for at in range(0, table.shape[1], line):
                    out[place : place + 1, :line] = table[i : i + 1, at : at + line]
                    place += 1


EXTRA = 16


def fold_body(keep, recv, send_out, keep_out):
    half = keep_out.shape[0]
    send_out[...] = keep[:half, :] + recv[:half, :]
    keep_out[...] = keep[half:, :] + recv[half:, :]


def add_body(keep, recv, out):
    out[...] = keep[...] + recv[...]


def add_two_body(first, second, third, out):
    out[...] = first[...] + (second[...] + third[...])


def fold_extra_body(keep, recv, send_out, keep_out):
    half = keep_out.shape[0] - EXTRA
    tables = keep[2 * half :, :] + recv[2 * half :, :]
    send_out[:half, :] = keep[:half, :] + recv[:half, :]
    keep_out[:half, :] = keep[half : 2 * half, :] + recv[half : 2 * half, :]
    send_out[half:, :] = tables
    keep_out[half:, :] = tables


class Bag:
    pass


class Sums:
    def __init__(self, chain, own, count, sources):
        self.chain, self.own, self.count, self.sources = chain, own, count, sources
        self.steps, self.flying, self.held, self.done = {}, {}, {}, {}
        self.extra = {}

    def outer(self, name, which):
        letters, segments = PIECES[name]
        bits = bits_of(letters, self.count)
        order = block_order(bits)
        half = self.count // 2
        offsets = order[which * half : (which + 1) * half]
        lefts = [self.sources[source][0] for source, _, _ in segments]
        rights = [self.sources[source][1] for source, _, _ in segments]
        size = lefts[0].shape[0] // self.count
        direct = size % 16 == 0
        if not direct:
            blocks = self.own[0] ^ jnp.array(offsets, jnp.int32)
            lefts = [
                left.reshape(self.count, size, -1)[blocks].reshape(half * size, -1) for left in lefts
            ]
        tables = self.extra.get(name, [])
        rows = half * size + (EXTRA if tables else 0)
        wide = sum(last - first for _, first, last in segments) * UNIT
        volume = sum(left.size * 3 for left in lefts) + sum(right.size * 2 for right in rights) + rows * wide * 8
        return self.chain(
            functools.partial(
                outer_body,
                parts=(len(segments), *((first, last) for _, first, last in segments)),
                offsets=offsets,
                size=size,
                direct=direct,
                tables=len(tables),
            ),
            (self.own, *lefts, *rights, *tables),
            [SMEM] + [VMEM] * (2 * len(segments) + len(tables)),
            (shape((rows, wide)),),
            (VMEM,),
            8 + volume // MIB,
            "outer_" + name + str(which),
            scratch=[pltpu.VMEM((half * size, left.shape[1]), LOW) for left in lefts] if direct else [],
        )[0]

    def fly(self, name, values):
        step = self.steps.get(name, 0)
        bits = bits_of(PIECES[name][0], self.count)
        self.flying[name] = swap(values, DP, self.count, bits[step])
        self.steps[name] = step + 1

    def send(self, name):
        self.fly(name, self.outer(name, 0))

    def keep(self, name):
        self.held[name] = self.outer(name, 1)

    def fold(self, name):
        if name in self.done:
            return
        keep, recv = self.held[name], self.flying[name]
        more = EXTRA if name in self.extra else 0
        rows = keep.shape[0] - more
        wide = keep.shape[1]
        if self.steps[name] == self.count.bit_length() - 1:
            (self.done[name],) = self.chain(
                add_body,
                (keep, recv),
                [VMEM, VMEM],
                (shape(keep.shape),),
                (VMEM,),
                4 + (keep.size * 12) // MIB,
                "last_" + name,
            )
        elif rows % 32:
            total = keep + recv
            tables = total[rows:]
            self.held[name] = jnp.concatenate([total[rows // 2 : rows], tables])
            self.fly(name, jnp.concatenate([total[: rows // 2], tables]))
        else:
            first, self.held[name] = self.chain(
                fold_extra_body if more else fold_body,
                (keep, recv),
                [VMEM, VMEM],
                (shape((rows // 2 + more, wide)),) * 2,
                (VMEM, VMEM),
                4 + (keep.size * 14) // MIB,
                "fold_" + name + str(self.steps[name]),
            )
            self.fly(name, first)

    def finish(self):
        while len(self.done) < len(PIECES):
            for name in PIECES:
                self.fold(name)


PLAN = (
    "ffn", "S:b", "S:a", "cross", "K:c", "K:b", "S:c", "self", "turnx", "K:a", "K:e", "S:e", "F:a",
    "F:b", "S:d", "in", "F:c", "F:e", "F:a", "K:d", "F:b", "F:d", "F:c", "store", "F:e", "F:a", "F:b",
    "F:c", "rest", "F:e", "F:d", "F:b", "F:c", "F:d", "F:a", "F:e", "F:d",
)


def per_device(
    count,
    inputs,
    datastore,
    lengths,
    indices,
    w_query,
    b_query,
    w_key,
    w_value,
    b_value,
    w_out,
    b_out,
    g_one,
    c_one,
    wc_query,
    bc_query,
    wc_key,
    wc_value,
    bc_value,
    wc_out,
    bc_out,
    g_two,
    c_two,
    w_up,
    b_up,
    w_down,
    b_down,
    g_three,
    c_three,
    cotangent,
):
    x = inputs[0]
    memory = datastore[0]
    q_scale = 1.0 / math.sqrt(HD)
    rank = lax.axis_index(DP).astype(jnp.int32)
    own = rank.reshape(1)
    side = lax.axis_index(TENSOR).astype(jnp.int32).reshape(1)
    chain = Chain()
    sources = {}
    sums = Sums(chain, own, count, sources)

    def other_core(values):
        return lax.ppermute(values, TENSOR, [(0, 1), (1, 0)])

    q, k, v, probs, inverse, ot, attended, self_part = self_forward(
        chain, lengths, x, w_query, b_query, w_key, w_value, b_value, w_out
    )
    self_other = other_core(self_part)
    words = mask_words(chain, indices[0])
    keys, values_t = store_products(chain, memory, wc_key, wc_value, True)
    unit_one, inv_one, one_t, cross_query, cross_probs, cross_sums, cross_ot, context, cross_part = cross_forward(
        chain, x, self_part, self_other, b_out, g_one, c_one, wc_query, bc_query, words, keys, values_t, bc_value, wc_out
    )
    cross_other = other_core(cross_part)
    values, keys_t = store_products(chain, memory, wc_key, wc_value, False)
    unit_two, inv_two, two_t, hidden, slope, ffn_part = ffn_forward(
        chain, unit_one, g_one, c_one, cross_part, cross_other, bc_out, g_two, c_two, w_up, b_up, w_down
    )
    ffn_other = other_core(ffn_part)
    memory_t = turn(chain, memory)
    output, grad_three, grad_ffn, ffn_t, sums_three = norm_three(
        chain, unit_two, g_two, c_two, ffn_part, ffn_other, b_down, g_three, c_three, cotangent[0]
    )
    sources["down"] = (ffn_t, hidden)
    half = memory.shape[0] // 2
    rows, wide = x.shape
    cols = w_query.shape[1]
    g = Bag()

    def do_ffn():
        g.pre, g.sums_up, g.two_part = ffn_backward(chain, grad_ffn, w_down, slope, w_up)
        g.two_other = other_core(g.two_part)
        sources["up"] = (two_t, g.pre)

    def do_cross():
        g.two, cross_t, g.sums_two, g.sums_cross, g.keys, g.values, asked, g.one_part = cross_backward(
            chain, grad_three, g.two_part, g.two_other, unit_two, inv_two, g_two, wc_out, cross_ot, cross_sums,
            cross_probs, values, keys_t, cross_query, wc_query,
        )
        g.one_other = other_core(g.one_part)
        sources["key"] = (memory_t, g.keys)
        sources["value"] = (memory_t, g.values)
        sources["mix"] = (cross_t, context)
        sources["ask"] = (one_t, asked)

    def do_self():
        g.one, self_t, sums_one, sums_self, grad_q, grad_k, grad_v, g.in_part = self_backward(
            chain, g.two, g.one_part, g.one_other, unit_one, inv_one, g_one, w_out, ot, inverse, probs,
            q, k, v, w_query, w_key, w_value,
        )
        g.in_other = other_core(g.in_part)
        g.q, g.k, g.v = grad_q, grad_k, grad_v
        sources["out"] = (self_t, attended)
        sums.extra[EXTRA_PIECE] = [sums_three, g.sums_two, sums_one, sums_self, g.sums_cross, g.sums_up]

    def do_turn_x():
        x_t = turn(chain, x)
        sources["q"] = (x_t, g.q)
        sources["k"] = (x_t, g.k)
        sources["v"] = (x_t, g.v)

    def do_in():
        block = pl.BlockSpec((rows // 2, wide), lambda i: (i, 0))
        (g.input,) = chain(
            add_two_body,
            (g.one, g.in_part, g.in_other),
            [block] * 3,
            (shape((rows, wide)),),
            (block,),
            20,
            "input_sum",
            grid=2,
        )

    def do_store():
        (part,) = chain(
            functools.partial(store_term_body, flipped=True),
            (side, g.keys, g.values, wc_key, wc_value),
            [SMEM] + [VMEM] * 4,
            (shape((half, wide)),),
            (VMEM,),
            20,
            "store_other",
        )
        g.store_other = other_core(part)

    def do_rest():
        (g.store,) = chain(
            store_sum_body,
            (side, g.keys, g.values, wc_key, wc_value, g.store_other),
            [SMEM] + [VMEM] * 5,
            (shape((half, wide)),),
            (VMEM,),
            24,
            "store_own",
        )

    jobs = {"turnx": do_turn_x, "ffn": do_ffn, "cross": do_cross, "self": do_self, "in": do_in, "store": do_store, "rest": do_rest}
    verbs = {"S": sums.send, "K": sums.keep, "F": sums.fold}
    for step in PLAN:
        verb, _, name = step.partition(":")
        if name:
            verbs[verb](name)
        else:
            jobs[verb]()
    sums.finish()
    input_grad = g.input[None]
    datastore_grad = g.store

    found = {}
    for name, (_, segments) in PIECES.items():
        start = 0
        for source, first, last in segments:
            span = (last - first) * UNIT
            found.setdefault(source, []).append(sums.done[name][: wide // count, start : start + span])
            start += span
    found = {source: jnp.concatenate(blocks, axis=1) for source, blocks in found.items()}
    table = sums.done[EXTRA_PIECE][wide // count :, :wide]
    mine = lax.dynamic_slice_in_dim(table[:9], rank * (wide // count), wide // count, axis=1)
    pairs = table[9:11].reshape(4, cols)
    pairs = lax.dynamic_slice_in_dim(pairs, rank * (cols // count), cols // count, axis=1)
    ups = table[11 : 11 + w_up.shape[1] // wide].reshape(-1)
    grad_b_up = lax.dynamic_slice_in_dim(ups, rank * (ups.shape[0] // count), ups.shape[0] // count)
    return (
        output[None],
        input_grad,
        datastore_grad[None],
        found["q"] * q_scale,
        pairs[0],
        found["k"],
        found["v"],
        pairs[1],
        found["out"].T,
        mine[8],
        mine[6],
        mine[7],
        found["ask"] * q_scale,
        pairs[3],
        found["key"],
        found["value"],
        pairs[2],
        found["mix"].T,
        mine[5],
        mine[3],
        mine[4],
        found["up"],
        grad_b_up,
        found["down"].T,
        mine[2],
        mine[0],
        mine[1],
    )


def solution(mesh):
    return jax.shard_map(
        functools.partial(per_device, mesh.shape[DP]),
        mesh=mesh,
        in_specs=(
            P(DP, None, None),
            P(DP, None, None),
            P(DP),
            P(DP, None, None),
            P(None, TENSOR),
            P(TENSOR),
            P(None, TENSOR),
            P(None, TENSOR),
            P(TENSOR),
            P(TENSOR, None),
            P(),
            P(),
            P(),
            P(None, TENSOR),
            P(TENSOR),
            P(None, TENSOR),
            P(None, TENSOR),
            P(TENSOR),
            P(TENSOR, None),
            P(),
            P(),
            P(),
            P(None, TENSOR),
            P(TENSOR),
            P(TENSOR, None),
            P(),
            P(),
            P(),
            P(DP, None, None),
        ),
        out_specs=(
            P(DP, None, None),
            P(DP, None, None),
            P(DP, TENSOR, None),
            P(DP, TENSOR),
            P((TENSOR, DP)),
            P(DP, TENSOR),
            P(DP, TENSOR),
            P((TENSOR, DP)),
            P(TENSOR, DP),
            P(DP),
            P(DP),
            P(DP),
            P(DP, TENSOR),
            P((TENSOR, DP)),
            P(DP, TENSOR),
            P(DP, TENSOR),
            P((TENSOR, DP)),
            P(TENSOR, DP),
            P(DP),
            P(DP),
            P(DP),
            P(DP, TENSOR),
            P((TENSOR, DP)),
            P(TENSOR, DP),
            P(DP),
            P(DP),
            P(DP),
        ),
        check_vma=False,
    )
```
